32 devices in a mesh: groups: 2 (over x), tensor: 4 (over y, core), rows: 4 (over z).
Axes of the slice: x: 2, y: 2, z: 4, core: 2. Of those that a mesh axis runs over, the one named last changes fastest.
Arguments:
- tokens: bfloat16 [2048, 8192], P(('groups', 'rows'), 'tensor'), parts along dimension 0, may hold values from -6 to 6
- norm_gain: bfloat16 [8192], replicated, may hold values from 0.099609375 to 1.8984375
- w_query: bfloat16 [8192, 4096], P(None, 'tensor'), may hold values from -0.0625 to 0.0625
- w_key: bfloat16 [8192, 512], P('tensor'), may hold values from -0.0625 to 0.0625
- w_value: bfloat16 [8192, 512], P('tensor'), may hold values from -0.0625 to 0.0625
- w_out: bfloat16 [4096, 8192], P('tensor'), may hold values from -0.75 to 0.75
- doc_ids: int32 [2048], P('groups'), parts along dimension 0, may hold values from 0 to 7, never falling along the last dimension, each value on 1 to 512 neighbouring positions
- assign: int32 [32, 1], P('groups'), parts along dimension 0, may hold values from 0 to 3; in each aligned block of 4 rows (0 to 3, 4 to 7, ...) at most 2 rows name the same one
- res_len: int32 [8], P('groups'), parts along dimension 0, may hold values from 1 to 512, 1280 in all
- res_mem: bfloat16 [8, 2, 512, 512], P(('groups', 'rows')), parts along dimension 0, may hold values from -160 to 160
Outputs:
- mixed: bfloat16 [2048, 8192], P(('groups', 'rows'), 'tensor'), parts along dimension 0
The draws below stay inside these ranges and needn't reach their ends.
There are 2 independent parts, one for each index of `groups`. The reference program is written for one: setup_inputs(seed, part) draws one part's arguments, and reference() takes and returns one part's arrays. A program takes and returns all parts, laid end to end along the dimension named above; an argument that names none is the same for every part. Nothing has to cross between parts.
Inputs may be any that keep to these rules, and one draw needn't show every extreme that they name: `doc_ids`: documents never fall along the pack; each holds at most 512 tokens and one holds exactly that many. `assign`: among the 4 blocks of one index of rows, no server is named more than 2 times.
All inputs are finite; a program needn't handle non-finite values.
Results may differ from the reference program's by a relative error of at most 0.017.
The reference program's roundings to bfloat16 on the way count: a program that leaves them out, or rounds other values in their place, can miss the bound.
Values may be sent and summed in bfloat16 or wider, within the bound.
No kernel may reach another device: no remote copies, remote signals or barrier semaphores. Data moves between devices by JAX's collectives and lax.ppermute only.
A program may use at most 128 MiB of HBM per device.

```python
import math
import jax
import jax.numpy as jnp
import numpy as np
from jax import lax

D = 8192
HQ = 32
KV = 4
HD = 128
TOK_DEV = 256
BLK = 64
CAP = 2
RES = 512
TOKENS = 1024
NB = 16
DOCS = 8
N_TENSOR = 4
N_ROWS = 4


def draw_res_mem(key, part):
    key = jax.random.fold_in(key, 7)
    values = jax.random.normal(key, (N_ROWS, 2, RES, KV * HD), jnp.float32)
    values = jnp.clip(values, -4.0, 4.0)
    return values.astype(jnp.bfloat16)


def level_of(own_key, dims, split, smallest, high):
    gain, own = 1.0, jax.random.fold_in(own_key, 6)
    for axis_at, blocks in split:
        steps = jnp.exp(jax.random.uniform(jax.random.fold_in(own, axis_at), (blocks,), jnp.float32, smallest / len(split), high / len(split)))
        gain = gain * jnp.repeat(steps, dims[axis_at] // blocks).reshape([-1 if axis == axis_at else 1 for axis in range(len(dims))])
    return gain


def profile(count, total, reach, skew):
    loads = [(1 << 20) // math.isqrt(standing ** skew) + 1 for standing in range(2, count + 1)]
    spare, counts = total - reach - (count - 1), [1] * (count - 1)
    while spare > 0:
        free = [i for i in range(count - 1) if counts[i] < reach]
        pool, remaining = sum([loads[i] for i in free]), spare
        for i in free:
            addition = min(reach - counts[i], max(1, remaining * loads[i] // pool), spare)
            counts[i] = counts[i] + addition
            spare = spare - addition
    return np.array([reach] + counts)


def uneven_parts(own_key, count, total, most, slope):
    if count == 2:
        one = jax.random.randint(own_key, (), max(1, total - most), min(most, total - 1) + 1)
        return jnp.stack([one, total - one])
    lengths = jnp.asarray(profile(count, total, most, slope), jnp.int32)
    pairs = (count - 1) // 2
    donor, receiver = lengths[1:1 + 2 * pairs:2], lengths[2:2 + 2 * pairs:2]
    slack = jnp.minimum(donor - 1, most - receiver)
    moved = jax.random.randint(jax.random.fold_in(own_key, 1), (pairs,), 0, 1 << 20) % (slack + 1)
    lengths = lengths.at[1:1 + 2 * pairs:2].set(donor - moved).at[2:2 + 2 * pairs:2].set(receiver + moved)
    return lengths[jax.random.permutation(jax.random.fold_in(own_key, 2), count)]


def assign_block(stream_key, own, number, rows, count, top, limit, skew):
    order = jax.random.permutation(stream_key, count)
    heavy_load, common = shares(count, rows * top, limit, skew, True), shares(count, rows * top, limit, skew, False)
    places = jnp.arange(count)

    def named(tallies, offset_by):
        used = int((tallies > 0).sum())
        fixed = max(1, used // 4)
        moved = fixed + (places - fixed + offset_by * (used - fixed)) % max(1, count - fixed)
        return jnp.zeros((count,), jnp.int32).at[order[jnp.where(places < fixed, places, moved)]].set(jnp.asarray(tallies, jnp.int32))

    tallies = jnp.where(number % 4 == 0, named(heavy_load, number // 4), named(common, number - number // 4 - 1))
    mixed = jax.random.permutation(jax.random.fold_in(own, 3), count)
    giver, receiver = mixed[0:count // 2 * 2:2], mixed[1:count // 2 * 2:2]
    margin = jnp.minimum(tallies[giver] - 1, limit - tallies[receiver]) // 2
    margin = jnp.where((giver == order[0]) | (receiver == order[0]) | (tallies[receiver] == 0), 0, jnp.maximum(margin, 0))
    moved = jax.random.randint(jax.random.fold_in(own, 4), (count // 2,), 0, 1 << 20) % (margin + 1)
    tallies = tallies.at[giver].add(-moved).at[receiver].add(moved)
    labels = jnp.searchsorted(jnp.cumsum(tallies), jnp.arange(rows * top), side="right").astype(jnp.int32)
    grid = labels.reshape(top, rows).T
    grid = grid[jax.random.permutation(jax.random.fold_in(own, 1), rows)]
    offset_by = jax.random.randint(jax.random.fold_in(own, 2), (rows, 1), 0, top)
    return jnp.take_along_axis(grid, (jnp.arange(top)[None, :] + offset_by) % top, axis=1)


def shares(number_of, total, most, lean, full):
    portions = [(1 << 20) // math.isqrt(standing ** lean) + 1 for standing in range(1, number_of + 1)]
    largest = most if full else min(most, max(-(-total // number_of), total * portions[0] // sum(portions)))
    least = 1 if total - largest >= number_of - 1 else 0
    given, rest = [largest] + [least] * (number_of - 1), total - largest - least * (number_of - 1)
    while rest > 0:
        candidates = [i for i in range(1, number_of) if given[i] < largest] or [i for i in range(1, number_of) if given[i] < most]
        whole, left = sum([portions[i] for i in candidates]), rest
        for i in candidates:
            more = min(most - given[i], max(1, left * portions[i] // whole), rest)
            given[i] = given[i] + more
            rest = rest - more
    return np.array(given)


def scatter_about(key, extent, width, limit, split=(), kind=jnp.bfloat16):
    values = width * jax.random.normal(key, extent, jnp.float32)
    if split:
        values = values * level_of(key, extent, split, -0.22, 0.18)
    return jnp.clip(values, -limit, limit).astype(kind)


def setup_inputs(seed: int = 0, part: int = 0) -> dict:
    keys = jax.random.split(jax.random.key(seed), 11)
    own_keys = jax.random.split(jax.random.fold_in(keys[10], part), 11)
    tokens = scatter_about(own_keys[0], (TOKENS, D), 1.0, 6.0, ((0, 4), (1, 4)))
    norm_gain = jnp.clip(1.0 + 0.18 * jax.random.normal(keys[1], (D,), jnp.float32), 0.099609375, 1.8984375).astype(jnp.bfloat16)
    w_query = scatter_about(keys[2], (D, HQ * HD), D ** -0.5, 0.0625, ((1, 4),))
    w_key = scatter_about(keys[3], (D, KV * HD), D ** -0.5, 0.0625, ((0, 4),))
    w_value = scatter_about(keys[4], (D, KV * HD), D ** -0.5, 0.0625, ((0, 4),))
    w_out = scatter_about(keys[5], (HQ * HD, D), (HQ * HD // 64) ** -0.5, 0.75, ((0, 4),))
    doc_ids = jnp.searchsorted(jnp.cumsum(uneven_parts(own_keys[6], DOCS, TOKENS, TOKENS // 2, 2)), jnp.arange(TOKENS), side="right").astype(jnp.int32)
    assign_keys = jax.random.split(jax.random.fold_in(own_keys[7], 1), NB // (TOK_DEV // BLK))
    assign_turns = jax.random.permutation(jax.random.fold_in(own_keys[7], 3), NB // (TOK_DEV // BLK))
    assign = jax.vmap(lambda own, number: assign_block(jax.random.fold_in(own_keys[7], 2), own, number, TOK_DEV // BLK, N_ROWS, 1, CAP, 2))(assign_keys, assign_turns).reshape((NB, 1))
    res_len = uneven_parts(own_keys[8], N_ROWS, (N_ROWS + 1) * RES // 2, RES, 2).astype(jnp.int32)
    res_mem = draw_res_mem(jax.random.fold_in(jax.random.fold_in(keys[10], part), 71), part)
    return {"tokens": tokens, "norm_gain": norm_gain, "w_query": w_query, "w_key": w_key, "w_value": w_value, "w_out": w_out, "doc_ids": doc_ids, "assign": assign, "res_len": res_len, "res_mem": res_mem}


norm_eps = 1e-05
rope_base = 500000.0
masked_score = -1e+30

def rotate(field, positions):
    half_dim = field.shape[-1] // 2
    frequency = rope_base ** (-(jnp.arange(half_dim, dtype=jnp.float32) / half_dim))
    angles = positions.astype(jnp.float32)[:, None] * frequency[None, :]
    cosine = jnp.cos(angles)[:, None, :]
    sine = jnp.sin(angles)[:, None, :]
    first = field[..., :half_dim]
    second = field[..., half_dim:]
    return jnp.concatenate([first * cosine - second * sine, first * sine + second * cosine], -1)

def reference(tokens, norm_gain, w_query, w_key, w_value, w_out, doc_ids, assign, res_len, res_mem):
    whole_f = tokens.astype(jnp.float32)
    normed = (whole_f * lax.rsqrt(lax.optimization_barrier(jnp.mean(whole_f * whole_f, -1, keepdims=True)) + norm_eps) * norm_gain.astype(jnp.float32)).astype(jnp.bfloat16)
    positions = jnp.arange(TOKENS, dtype=jnp.int32)
    query = rotate(jnp.dot(normed, w_query, preferred_element_type=jnp.float32).reshape(TOKENS, HQ, HD), positions).astype(jnp.bfloat16)
    key_rows = rotate(jnp.dot(normed, w_key, preferred_element_type=jnp.float32).reshape(TOKENS, KV, HD), positions).astype(jnp.bfloat16)
    value_rows = jnp.dot(normed, w_value, preferred_element_type=jnp.float32).reshape(TOKENS, KV, HD).astype(jnp.bfloat16)
    group_size = HQ // KV
    score_scale = 1.0 / math.sqrt(HD)
    key_float = key_rows.astype(jnp.float32)
    value_float = value_rows.astype(jnp.float32)

    def one_block(index):
        server = assign[index, 0]
        block_query = lax.dynamic_slice_in_dim(query, index * BLK, BLK, 0).reshape(BLK, KV, group_size, HD).astype(jnp.float32)
        q_pos = index * BLK + jnp.arange(BLK, dtype=jnp.int32)
        q_doc = lax.dynamic_slice_in_dim(doc_ids, index * BLK, BLK, 0)
        memory = lax.dynamic_index_in_dim(res_mem, server, 0, keepdims=False).astype(jnp.float32)
        mem_keys = memory[0].reshape(RES, KV, HD)
        mem_values = memory[1].reshape(RES, KV, HD)
        doc_scores = jnp.einsum('xkgd,tkd->kgxt', block_query, key_float) * score_scale
        doc_mask = (doc_ids[None, :] == q_doc[:, None]) & (jnp.arange(TOKENS, dtype=jnp.int32)[None, :] <= q_pos[:, None])
        doc_scores = jnp.where(doc_mask[None, None], doc_scores, masked_score)
        mem_scores = jnp.einsum('xkgd,mkd->kgxm', block_query, mem_keys) * score_scale
        mem_mask = jnp.arange(RES, dtype=jnp.int32) < res_len[server]
        mem_scores = jnp.where(mem_mask[None, None, None, :], mem_scores, masked_score)
        row_max = jnp.maximum(lax.optimization_barrier(jnp.max(doc_scores, -1)), lax.optimization_barrier(jnp.max(mem_scores, -1)))[..., None]
        doc_exp = jnp.exp(doc_scores - row_max)
        mem_exp = jnp.exp(mem_scores - row_max)
        row_total = lax.optimization_barrier(jnp.sum(doc_exp, -1, keepdims=True)) + lax.optimization_barrier(jnp.sum(mem_exp, -1, keepdims=True))
        doc_weights = lax.optimization_barrier((doc_exp / row_total).astype(jnp.bfloat16)).astype(jnp.float32)
        mem_weights = lax.optimization_barrier((mem_exp / row_total).astype(jnp.bfloat16)).astype(jnp.float32)
        mixed = jnp.einsum('kgxt,tkd->xkgd', doc_weights, value_float) + jnp.einsum('kgxm,mkd->xkgd', mem_weights, mem_values)
        return mixed.astype(jnp.bfloat16).reshape(BLK, HQ * HD)
    attended = lax.map(one_block, jnp.arange(NB, dtype=jnp.int32)).reshape(TOKENS, HQ * HD)
    columns = HQ * HD // N_TENSOR
    head_parts = attended.reshape(TOKENS, N_TENSOR, columns).transpose(1, 0, 2)
    weight_parts = w_out.reshape(N_TENSOR, columns, D)

    def add_term(total, pieces):
        term = jnp.dot(pieces[0], pieces[1], preferred_element_type=jnp.float32)
        rounded = lax.optimization_barrier(term.astype(jnp.bfloat16)).astype(jnp.float32)
        return (total + rounded, None)
    summed, unused = lax.scan(add_term, jnp.zeros((TOKENS, D), jnp.float32), (head_parts, weight_parts))
    return summed.astype(jnp.bfloat16)
```

```python
import functools
import math

import jax
import jax.numpy as jnp
from jax import lax
from jax.experimental import pallas as pl
from jax.experimental.pallas import tpu as pltpu
from jax.sharding import PartitionSpec as P

HD = 128
BLK = 64
HALVES = 2

norm_eps = 1e-05
rope_base = 500000.0
masked_score = -1e30
MIB = 1 << 20
f32 = jnp.float32
bf16 = jnp.bfloat16
NT = (((1,), (1,)), ((), ()))


def params(mib):
    return pltpu.CompilerParams(vmem_limit_bytes=mib * MIB)


def whole(shape):
    return pl.BlockSpec(shape, lambda *_: (0,) * len(shape))


def cost(flops, moved, exps=0):
    return pl.CostEstimate(flops=flops, bytes_accessed=moved, transcendentals=exps)


def prep_kernel(x_ref, *out_refs):
    stat_ref = out_refs[-1]
    rows, width = x_ref.shape
    part = rows // (len(out_refs) - 1)
    for at, out_ref in enumerate(out_refs[:-1]):
        out_ref[...] = x_ref[at * part : (at + 1) * part, :]
    lanes = jnp.zeros((rows, HD), f32)
    for at in range(width // HD):
        piece = x_ref[:, at * HD : (at + 1) * HD].astype(f32)
        lanes = lanes + piece * piece
    total = jnp.sum(lanes, -1, keepdims=True)
    stat_ref[...] = jnp.broadcast_to(total, (rows, HD)).T[:8, :]


def prep(tokens):
    rows, width = tokens.shape
    halves = [jax.ShapeDtypeStruct((rows // HALVES, width), bf16)] * HALVES
    return pl.pallas_call(
        prep_kernel,
        out_shape=halves + [jax.ShapeDtypeStruct((8, rows), f32)],
        compiler_params=params(16),
        cost_estimate=cost(2 * rows * width, 4 * rows * width),
        name="prep",
    )(tokens)


def inverse_rms(stat_refs, features):
    total = stat_refs[0][...]
    for ref in stat_refs[1:]:
        total = total + ref[...]
    return lax.rsqrt(total / features + norm_eps).T[:, :1]


def normalise(x, inverse, gain):
    return (x.astype(f32) * inverse * gain.astype(f32)).astype(bf16)


def kv_kernel(heads_ref, features, n_stats, *refs):
    stats = refs[:n_stats]
    x_ref, gain_ref, wk_ref, wv_ref, own_ref, send_ref, acc_k, acc_v, inv_ref = refs[n_stats:]
    step = pl.program_id(0)

    @pl.when(step == 0)
    def _():
        inv_ref[...] = jnp.broadcast_to(inverse_rms(stats, features), inv_ref.shape)
        acc_k[...] = jnp.zeros_like(acc_k)
        acc_v[...] = jnp.zeros_like(acc_v)

    normed = normalise(x_ref[...], inv_ref[:, :1], gain_ref[0])
    acc_k[...] += jnp.dot(normed, wk_ref[...], preferred_element_type=f32)
    acc_v[...] += jnp.dot(normed, wv_ref[...], preferred_element_type=f32)

    @pl.when(step == pl.num_programs(0) - 1)
    def _():
        chips = own_ref.shape[0]
        for at, out_ref in enumerate((own_ref, send_ref)):
            for chip in range(chips):
                head = heads_ref[at * chips + chip]
                columns = pl.ds(pl.multiple_of(head * HD, HD), HD)
                out_ref[chip, :, :HD] = acc_k[:, columns].astype(bf16)
                out_ref[chip, :, HD:] = acc_v[:, columns].astype(bf16)


def kv_partial(heads, stats, tokens, gain, w_key, w_value, me, features, chips):
    rows, width = tokens.shape
    kv_width = w_key.shape[1]
    tile = min(width, 512)
    steps = width // tile
    out = jax.ShapeDtypeStruct((chips, rows, 2 * HD), bf16)

    def body(scalars, *refs):
        kv_kernel(scalars, features, len(stats), *refs)

    gains = gain.reshape(features // tile, 1, tile)
    scalars = jnp.concatenate([heads, me[None]]).astype(jnp.int32)
    return pl.pallas_call(
        body,
        out_shape=[out, out],
        grid_spec=pltpu.PrefetchScalarGridSpec(
            num_scalar_prefetch=1,
            grid=(steps,),
            in_specs=[whole((8, rows))] * len(stats)
            + [
                pl.BlockSpec((rows, tile), lambda k, s: (0, k)),
                pl.BlockSpec((1, 1, tile), lambda k, s: (s[2 * chips] * steps + k, 0, 0)),
                pl.BlockSpec((tile, kv_width), lambda k, s: (k, 0)),
                pl.BlockSpec((tile, kv_width), lambda k, s: (k, 0)),
            ],
            out_specs=[whole(out.shape)] * 2,
            scratch_shapes=[
                pltpu.VMEM((rows, kv_width), f32),
                pltpu.VMEM((rows, kv_width), f32),
                pltpu.VMEM((rows, HD), f32),
            ],
        ),
        compiler_params=params(24),
        cost_estimate=cost(4 * rows * width * kv_width, 4 * width * kv_width + 2 * rows * width),
        name="kv_partial",
    )(scalars, *stats, tokens, gains, w_key, w_value)


def turn(x, cosine, sine):
    return x * cosine + pltpu.roll(x, HD // 2, 1) * sine


def kv_final(own, arrived, others, cosine, sine, chip):
    _, rows, width = own.shape

    def body(chip_ref, own_ref, arrived_ref, *refs):
        cos_ref, sin_ref, out_ref = refs[-3:]
        total = own_ref[0].astype(f32) + arrived_ref[0].astype(f32)
        for ref in refs[:-3]:
            total = total + ref[...].astype(f32)
        out_ref[:, :HD] = turn(total[:, :HD], cos_ref[...], sin_ref[...]).astype(bf16)
        out_ref[:, HD:] = total[:, HD:].astype(bf16)

    mine = pl.BlockSpec((1, rows, width), lambda i, s: (s[0], 0, 0))
    return pl.pallas_call(
        body,
        out_shape=jax.ShapeDtypeStruct((rows, width), bf16),
        grid_spec=pltpu.PrefetchScalarGridSpec(
            num_scalar_prefetch=1,
            grid=(1,),
            in_specs=[mine, mine]
            + [whole((rows, width))] * len(others)
            + [whole((rows, HD))] * 2,
            out_specs=whole((rows, width)),
        ),
        compiler_params=params(16),
        cost_estimate=cost(8 * rows * width, 8 * rows * width),
        name="kv_final",
    )(chip[None], own, arrived, *others, cosine, sine)


def query_kernel(order_ref, features, n_stats, n_sources, per_source, *refs):
    stats = refs[:n_stats]
    sources = refs[n_stats : n_stats + n_sources]
    gain_ref, w_ref, cos_ref, sin_ref, out_ref, acc_ref, inv_ref = refs[n_stats + n_sources :]
    step = pl.program_id(0)

    @pl.when(step == 0)
    def _():
        inv_ref[...] = jnp.broadcast_to(inverse_rms(stats, features), inv_ref.shape)
        acc_ref[...] = jnp.zeros_like(acc_ref)

    for at, x_ref in enumerate(sources):

        @pl.when(step // per_source == at)
        def _():
            normed = normalise(x_ref[...], inv_ref[:, :1], gain_ref[0])
            acc_ref[...] += jnp.dot(normed, w_ref[...], preferred_element_type=f32)

    @pl.when(step == pl.num_programs(0) - 1)
    def _():
        for head in range(out_ref.shape[1] // HD):
            columns = slice(head * HD, (head + 1) * HD)
            rotated = turn(acc_ref[:, columns], cos_ref[...], sin_ref[...])
            out_ref[:, columns] = rotated.astype(bf16)


def query_half(half, order, stats, sources, gain, w_query, cosine, sine):
    rows, width = sources[0].shape
    features, columns = w_query.shape
    tile = min(width, 1024)
    per_source = width // tile

    def body(order_ref, *refs):
        query_kernel(order_ref, features, len(stats), len(sources), per_source, *refs)

    def source_spec(at):
        return pl.BlockSpec(
            (rows, tile), lambda k, s: (0, jnp.clip(k - at * per_source, 0, per_source - 1))
        )

    def place(k, s):
        return s[k // per_source] * per_source + k % per_source

    table = pl.BlockSpec((rows, HD), lambda k, s: (half, 0))
    return pl.pallas_call(
        body,
        out_shape=jax.ShapeDtypeStruct((rows, columns), bf16),
        grid_spec=pltpu.PrefetchScalarGridSpec(
            num_scalar_prefetch=1,
            grid=(features // tile,),
            in_specs=[pl.BlockSpec((8, rows), lambda k, s: (0, half))] * len(stats)
            + [source_spec(at) for at in range(len(sources))]
            + [
                pl.BlockSpec((1, 1, tile), lambda k, s: (place(k, s), 0, 0)),
                pl.BlockSpec((tile, columns), lambda k, s: (place(k, s), 0)),
                table,
                table,
            ],
            out_specs=whole((rows, columns)),
            scratch_shapes=[pltpu.VMEM((rows, columns), f32), pltpu.VMEM((rows, HD), f32)],
        ),
        compiler_params=params(24),
        cost_estimate=cost(2 * rows * features * columns, 2 * features * columns),
        name="query_half",
    )(order, *stats, *sources, gain.reshape(features // tile, 1, tile), w_query, cosine, sine)


def attend_kernel(half, pick_ref, q_ref, qdoc_ref, kdoc_ref, *refs):
    rows, columns = q_ref.shape
    heads = columns // HD
    n_kv = kdoc_ref.shape[1] // refs[0].shape[0]
    out_ref = refs[-1]
    kv_refs, mem_refs = refs[:n_kv], refs[n_kv:-1]
    rows_dev = kv_refs[0].shape[0]
    back = (n_kv - 1) * rows_dev
    low, high = half * rows, back + (half + 1) * rows
    keys, values = [], []
    for at, ref in enumerate(kv_refs):
        first, last = max(low, at * rows_dev), min(high, (at + 1) * rows_dev)
        if first < last:
            part = slice(first - at * rows_dev, last - at * rows_dev)
            keys.append(ref[part, :HD])
            values.append(ref[part, HD:])
    keys, values = jnp.concatenate(keys, 0), jnp.concatenate(values, 0)
    span = high - low
    scale = math.log2(math.e) / math.sqrt(HD)
    blocks = rows // BLK
    for block in range(blocks):
        tokens = slice(block * BLK, (block + 1) * BLK)
        query = jnp.concatenate(
            [q_ref[tokens, h * HD : (h + 1) * HD] for h in range(heads)], 0
        )
        slot = pick_ref[block]
        mem_keys, mem_values = mem_refs[0][0], mem_refs[0][1]
        for at, ref in enumerate(mem_refs[1:]):
            mem_keys = jnp.where(slot == at + 1, ref[0], mem_keys)
            mem_values = jnp.where(slot == at + 1, ref[1], mem_values)
        column = lax.broadcasted_iota(jnp.int32, (BLK, span), 1)
        row = lax.broadcasted_iota(jnp.int32, (BLK, span), 0)
        mask = (column - back <= row + block * BLK) & (
            kdoc_ref[:, low:high] == qdoc_ref[tokens, :1]
        )
        live = lax.broadcasted_iota(jnp.int32, (1, mem_keys.shape[0]), 1) < pick_ref[blocks + block]
        doc = lax.dot_general(query, keys, NT, preferred_element_type=f32)
        mem = lax.dot_general(query, mem_keys, NT, preferred_element_type=f32)
        doc = jnp.where(mask[None], (doc * scale).reshape(heads, BLK, span), masked_score)
        doc = doc.reshape(heads * BLK, span)
        mem = jnp.where(live, mem * scale, masked_score)
        top = jnp.maximum(jnp.max(doc, -1, keepdims=True), jnp.max(mem, -1, keepdims=True))
        doc, mem = jnp.exp2(doc - top), jnp.exp2(mem - top)
        total = jnp.sum(doc, -1, keepdims=True) + jnp.sum(mem, -1, keepdims=True)
        share = 1.0 / total
        mixed = jnp.dot((doc * share).astype(bf16), values, preferred_element_type=f32)
        mixed = mixed + jnp.dot(
            (mem * share).astype(bf16), mem_values, preferred_element_type=f32
        )
        mixed = mixed.astype(bf16)
        for h in range(heads):
            out_ref[tokens, h * HD : (h + 1) * HD] = mixed[h * BLK : (h + 1) * BLK]


def attend_half(half, pick, query, q_doc, k_doc, kv, memories):
    rows, columns = query.shape
    slots = memories[0].shape
    span = k_doc.shape[1] + slots[1]
    return pl.pallas_call(
        functools.partial(attend_kernel, half),
        out_shape=jax.ShapeDtypeStruct(query.shape, bf16),
        grid_spec=pltpu.PrefetchScalarGridSpec(
            num_scalar_prefetch=1,
            grid=(1,),
            in_specs=[
                whole((rows, columns)),
                pl.BlockSpec((rows, HD), lambda i, s: (half, 0)),
                whole(k_doc.shape),
            ]
            + [whole(kv[0].shape)] * len(kv)
            + [whole(slots)] * len(memories),
            out_specs=whole((rows, columns)),
        ),
        compiler_params=params(40),
        cost_estimate=cost(
            4 * rows * columns * span, 4 * rows * columns, rows * columns // HD * span
        ),
        name="attend_half",
    )(pick, query, q_doc, k_doc, *kv, *memories)


def project(attended, w_out, target, width, added=(), kind=bf16):
    rows, depth = attended.shape
    tile = min(width, 512)
    steps = width // tile

    def body(target_ref, a_ref, w_ref, *refs):
        total = jnp.dot(a_ref[...], w_ref[...], preferred_element_type=f32)
        for ref in refs[:-1]:
            total = total + ref[...].astype(f32)
        refs[-1][...] = total.astype(kind)

    piece = pl.BlockSpec((rows, tile), lambda k, s: (0, k))
    return pl.pallas_call(
        body,
        out_shape=jax.ShapeDtypeStruct((rows, width), kind),
        grid_spec=pltpu.PrefetchScalarGridSpec(
            num_scalar_prefetch=1,
            grid=(steps,),
            in_specs=[
                whole((rows, depth)),
                pl.BlockSpec((depth, tile), lambda k, s: (0, s[0] * steps + k)),
            ]
            + [piece] * len(added),
            out_specs=piece,
        ),
        compiler_params=params(16),
        cost_estimate=cost(2 * rows * depth * width, 2 * depth * width),
        name="project",
    )(target[None], attended, w_out, *added)


def on_device(tokens, norm_gain, w_query, w_key, w_value, w_out, doc_ids, assign, res_len, res_mem):
    n_tensor = lax.axis_size("tensor")
    n_rows = lax.axis_size("rows")
    chips = n_tensor // 2
    tensor_index = lax.axis_index("tensor").astype(jnp.int32)
    row_index = lax.axis_index("rows").astype(jnp.int32)
    chip, core = tensor_index // 2, tensor_index % 2
    rows_dev, width = tokens.shape
    features = norm_gain.shape[0]
    kv_heads = w_key.shape[1] // HD
    sharers = n_tensor // kv_heads

    def to_core(x):
        return lax.ppermute(x, "tensor", [(i, i ^ 1) for i in range(n_tensor)])

    def to_chip(x, ahead):
        pairs = [(i, (i + 2 * ahead) % n_tensor) for i in range(n_tensor)]
        return lax.ppermute(x, "tensor", pairs)

    def up(x):
        return lax.ppermute(x, "rows", [(i, i + 1) for i in range(n_rows - 1)])

    def down(x):
        return lax.ppermute(x, "rows", [(i + 1, i) for i in range(n_rows - 1)])

    away = range(1, chips)

    *halves, stat = prep(tokens)
    chip_stats = [to_chip(stat, ahead) for ahead in away]
    stats = [stat, to_core(stat)] + chip_stats + [to_core(s) for s in chip_stats]
    sources = []
    for part in halves:
        arrived = [to_chip(part, ahead) for ahead in away]
        sources.append([part, to_core(part)] + arrived + [to_core(a) for a in arrived])
    order = [tensor_index, tensor_index ^ 1]
    order += [(tensor_index - 2 * ahead) % n_tensor for ahead in away]
    order += [((tensor_index ^ 1) - 2 * ahead) % n_tensor for ahead in away]
    order = jnp.stack(order).astype(jnp.int32)

    head_group = tensor_index // sharers
    memory = lax.dynamic_slice_in_dim(res_mem[0], head_group * HD, HD, 2)
    memories, rising, falling = [memory], memory, memory
    lifted, lowered = [], []
    for _ in range(n_rows - 1):
        rising, falling = up(rising), down(falling)
        lifted.append(rising)
        lowered.append(falling)
    memories = [memory] + lifted + lowered

    positions = (row_index * rows_dev + jnp.arange(rows_dev, dtype=jnp.int32)).astype(f32)
    half_dim = HD // 2
    frequency = rope_base ** (-(jnp.arange(half_dim, dtype=f32) / half_dim))
    angles = positions[:, None] * frequency[None, :]
    cosine, sine = jnp.cos(angles), jnp.sin(angles)
    cosine = jnp.concatenate([cosine, cosine], 1)
    sine = jnp.concatenate([-sine, sine], 1)

    targets = jnp.arange(chips, dtype=jnp.int32) * 2
    heads = jnp.concatenate([(targets + core) // sharers, (targets + 1 - core) // sharers])
    own, send = kv_partial(
        heads, stats, tokens, norm_gain, w_key, w_value, tensor_index, features, chips
    )
    arrived = to_core(send)
    others = []
    for ahead in away:
        target = (chip + ahead) % chips
        pair = lax.dynamic_index_in_dim(own, target, 0, False).astype(f32)
        pair = pair + lax.dynamic_index_in_dim(arrived, target, 0, False).astype(f32)
        others.append(to_chip(pair.astype(bf16), ahead))
    kv = [kv_final(own, arrived, others, cosine, sine, chip)]
    total_rows = n_rows * rows_dev
    longest = total_rows // 2
    back = -(-(longest - 1) // rows_dev)
    for _ in range(back):
        kv.insert(0, up(kv[0]))

    padded = jnp.concatenate([jnp.full((back * rows_dev,), -1, jnp.int32), doc_ids])
    k_doc = lax.dynamic_slice_in_dim(padded, row_index * rows_dev, (back + 1) * rows_dev)[None]
    q_doc = jnp.broadcast_to(k_doc[0, back * rows_dev :, None], (rows_dev, HD))
    blocks_dev = rows_dev // BLK
    servers = lax.dynamic_slice_in_dim(assign[:, 0], row_index * blocks_dev, blocks_dev)
    apart = row_index - servers
    slots = jnp.where(apart >= 0, apart, n_rows - 1 - apart).astype(jnp.int32)
    lives = res_len[servers].astype(jnp.int32)
    per_half = blocks_dev // HALVES

    outs = []
    for half in range(HALVES):
        query = query_half(half, order, stats, sources[half], norm_gain, w_query, cosine, sine)
        mine = slice(half * per_half, (half + 1) * per_half)
        pick = jnp.concatenate([slots[mine], lives[mine]])
        attended = attend_half(half, pick, query, q_doc, k_doc, kv, memories)
        arrived = []
        for ahead in away:
            far = ((chip + ahead) % chips) * 2
            other = to_core(project(attended, w_out, far + 1 - core, width))
            pair = project(attended, w_out, far + core, width, (other,))
            arrived.append(to_chip(pair, ahead))
        near = to_core(project(attended, w_out, tensor_index ^ 1, width))
        part = project(attended, w_out, tensor_index, width, (near,), f32)
        for piece in arrived:
            part = part + piece.astype(f32)
        outs.append(part.astype(bf16))
    return jnp.concatenate(outs, 0)


def solution(mesh):
    in_specs = (
        P(("groups", "rows"), "tensor"),
        P(),
        P(None, "tensor"),
        P("tensor", None),
        P("tensor", None),
        P("tensor", None),
        P("groups"),
        P("groups", None),
        P("groups"),
        P(("groups", "rows"), None, None, None),
    )
    out_specs = P(("groups", "rows"), "tensor")
    return jax.shard_map(
        on_device, mesh=mesh, in_specs=in_specs, out_specs=out_specs, check_vma=False
    )
```

```python
import functools
import math

import jax
import jax.numpy as jnp
from jax import lax
from jax.experimental import pallas as pl
from jax.experimental.pallas import tpu as pltpu
from jax.sharding import PartitionSpec as P

HD = 128
BLK = 64
HALVES = 2
STREAMS = 8
CHEAP = 100
DEPTH = 6

norm_eps = 1e-05
rope_base = 500000.0
masked_score = -1e30
MIB = 1 << 20
f32 = jnp.float32
bf16 = jnp.bfloat16
NT = (((1,), (1,)), ((), ()))


def params(mib):
    return pltpu.CompilerParams(vmem_limit_bytes=mib * MIB)


def whole(shape):
    return pl.BlockSpec(shape, lambda *_: (0,) * len(shape))


def resident(x):
    return pltpu.with_memory_space_constraint(x, pltpu.VMEM)


def placed(space, shape):
    return space(shape, bf16)


def in_hbm(x):
    return pltpu.with_memory_space_constraint(x, pltpu.HBM)


VMEM = pl.BlockSpec(memory_space=pltpu.VMEM)
ANY = pl.BlockSpec(memory_space=pl.ANY)


def after(x, *first):
    return lax.optimization_barrier((x, *first))[0]


def cost(flops, moved, exps=0):
    return pl.CostEstimate(
        flops=flops // CHEAP, bytes_accessed=moved // CHEAP, transcendentals=exps // CHEAP
    )


def streamed(copies, at, depth=DEPTH):
    if at == 0:
        for copy in copies[:depth]:
            copy.start()
    copies[at].wait()
    if at + depth < len(copies):
        copies[at + depth].start()


def prep(tokens, sizes):
    rows, width = tokens.shape
    count, parts = len(sizes), 4
    size = rows // parts

    def body(x_ref, *refs):
        *out_refs, held_ref, stat_ref, sems = refs
        firsts = [at * size for at in range(parts)]
        reads = []
        for at, first in enumerate(firsts):
            part = pl.ds(first, size)
            reads.append(
                pltpu.make_async_copy(x_ref.at[part, :], held_ref.at[part, :], sems.at[at])
            )
            reads[at].start()
        begin, copies, totals = 0, [], []
        for at, first in enumerate(firsts):
            reads[at].wait()
            while len(copies) < count and begin + sizes[len(copies)] <= first + size:
                part = pl.ds(begin, sizes[len(copies)])
                sem = sems.at[parts + len(copies)]
                out_ref = out_refs[len(copies)]
                begin += sizes[len(copies)]
                copies.append(pltpu.make_async_copy(held_ref.at[part, :], out_ref, sem))
                copies[-1].start()
            lanes = jnp.zeros((size, HD), f32)
            for k in range(width // HD):
                piece = held_ref[first : first + size, k * HD : (k + 1) * HD].astype(f32)
                lanes = lanes + piece * piece
            totals.append(jnp.sum(lanes, -1, keepdims=True))
        total = jnp.concatenate(totals, 0)
        stat_ref[...] = jnp.broadcast_to(total, (rows, HD)).T[:8, :]
        for copy in copies:
            copy.wait()

    return pl.pallas_call(
        body,
        out_shape=[placed(pltpu.HBM, (piece, width)) for piece in sizes]
        + [placed(pltpu.VMEM, (rows, width)), jax.ShapeDtypeStruct((8, rows), f32)],
        in_specs=[ANY],
        out_specs=[ANY] * count + [VMEM] * 2,
        scratch_shapes=[pltpu.SemaphoreType.DMA((parts + count,))],
        compiler_params=params(2),
        cost_estimate=cost(2 * rows * width, 4 * rows * width),
        name="prep",
    )(in_hbm(tokens))


def inverse_rms(stat_refs, features):
    total = stat_refs[0][...]
    for ref in stat_refs[1:]:
        total = total + ref[...]
    return lax.rsqrt(total / features + norm_eps).T[:, :1]


def normalise(x, inverse, gain):
    return (x.astype(f32) * inverse * gain).astype(bf16)


def load(arrays):
    def body(*refs):
        count = len(arrays)
        sems = refs[-1]
        copies = [
            pltpu.make_async_copy(refs[at], refs[count + at], sems.at[at]) for at in range(count)
        ]
        for copy in copies:
            copy.start()
        for copy in copies:
            copy.wait()

    moved = sum(a.size * 2 for a in arrays)
    return pl.pallas_call(
        body,
        out_shape=[placed(pltpu.VMEM, a.shape) for a in arrays],
        in_specs=[ANY] * len(arrays),
        out_specs=[VMEM] * len(arrays),
        scratch_shapes=[pltpu.SemaphoreType.DMA((len(arrays),))],
        compiler_params=params(2),
        cost_estimate=cost(0, moved),
        name="load",
    )(*[in_hbm(a) for a in arrays])


def kv_partial(scalars, stats, gain, tokens, w_key, w_value, chips):
    rows, width = tokens.shape
    features = gain.shape[1]
    kv_width = w_key.shape[1]
    tile = min(width, 512)
    out = jax.ShapeDtypeStruct((chips, rows, 2 * HD), bf16)

    def body(scalars_ref, *refs):
        gain_ref, x_ref, wk_ref, wv_ref, own_ref, send_ref, acc_k, acc_v = refs[len(stats) :]
        inverse = inverse_rms(refs[: len(stats)], features)
        base = scalars_ref[2 * chips] * width
        for k in range(width // tile):
            part = slice(k * tile, (k + 1) * tile)
            gains = gain_ref[:, pl.ds(pl.multiple_of(base + k * tile, tile), tile)]
            normed = normalise(x_ref[:, part], inverse, gains)
            keys = jnp.dot(normed, wk_ref[part, :], preferred_element_type=f32)
            values = jnp.dot(normed, wv_ref[part, :], preferred_element_type=f32)
            acc_k[...] = keys if k == 0 else acc_k[...] + keys
            acc_v[...] = values if k == 0 else acc_v[...] + values
        for at, out_ref in enumerate((own_ref, send_ref)):
            for chip in range(chips):
                head = scalars_ref[at * chips + chip]
                columns = pl.ds(pl.multiple_of(head * HD, HD), HD)
                out_ref[chip, :, :HD] = acc_k[:, columns].astype(bf16)
                out_ref[chip, :, HD:] = acc_v[:, columns].astype(bf16)

    return pl.pallas_call(
        body,
        out_shape=[out, out],
        grid_spec=pltpu.PrefetchScalarGridSpec(
            num_scalar_prefetch=1,
            grid=(1,),
            in_specs=[VMEM] * (len(stats) + 4),
            out_specs=[VMEM] * 2,
            scratch_shapes=[pltpu.VMEM((rows, kv_width), f32)] * 2,
        ),
        compiler_params=params(8),
        cost_estimate=cost(4 * rows * width * kv_width, 2 * rows * width),
        name="kv_partial",
    )(scalars, *stats, gain, resident(tokens), resident(w_key), resident(w_value))


def turn(x, cosine, sine):
    return x * cosine + pltpu.roll(x, HD // 2, 1) * sine


def kv_final(own, arrived, others, cosine, sine, chip):
    _, rows, width = own.shape

    def body(chip_ref, own_ref, arrived_ref, *refs):
        cos_ref, sin_ref, out_ref = refs[-3:]
        total = own_ref[0].astype(f32) + arrived_ref[0].astype(f32)
        for ref in refs[:-3]:
            total = total + ref[...].astype(f32)
        out_ref[:, :HD] = turn(total[:, :HD], cos_ref[...], sin_ref[...]).astype(bf16)
        out_ref[:, HD:] = total[:, HD:].astype(bf16)

    mine = pl.BlockSpec((1, rows, width), lambda i, s: (s[0], 0, 0))
    return pl.pallas_call(
        body,
        out_shape=jax.ShapeDtypeStruct((rows, width), bf16),
        grid_spec=pltpu.PrefetchScalarGridSpec(
            num_scalar_prefetch=1,
            grid=(1,),
            in_specs=[mine, mine]
            + [whole((rows, width))] * len(others)
            + [whole((rows, HD))] * 2,
            out_specs=whole((rows, width)),
        ),
        compiler_params=params(16),
        cost_estimate=cost(8 * rows * width, 8 * rows * width),
        name="kv_final",
    )(chip[None], own, arrived, *others, cosine, sine)


def query_near(scalars, stats, gain, own, other, w_query):
    rows, width = own.shape
    features, columns = gain.shape[1], w_query.shape[1]
    steps = max(2, STREAMS)
    tile = 2 * width // steps
    n_stats = len(stats)

    def body(scalars_ref, *refs):
        gain_ref, own_ref, other_ref, w_ref, out_ref, x_held, w_held, sems, x_sem = refs[n_stats:]
        other_copy = pltpu.make_async_copy(other_ref, x_held, x_sem)
        places, copies = [], []
        for k in range(steps):
            base = scalars_ref[k * tile // width] * width + k * tile % width
            places.append(pl.ds(pl.multiple_of(base, tile), tile))
            held = w_held.at[pl.ds(k * tile, tile), :]
            copies.append(pltpu.make_async_copy(w_ref.at[places[k], :], held, sems.at[k]))
        inverse = None
        for k in range(steps):
            first = k * tile % width
            if k == steps // 2:
                other_copy.wait()
            streamed(copies, k)
            if k == 0:
                other_copy.start()
                inverse = inverse_rms(refs[:n_stats], features)
            piece = (own_ref if k < steps // 2 else x_held)[:, first : first + tile]
            normed = normalise(piece, inverse, gain_ref[:, places[k]])
            term = jnp.dot(
                normed, w_held[k * tile : (k + 1) * tile, :], preferred_element_type=f32
            )
            out_ref[...] = term if k == 0 else out_ref[...] + term

    return pl.pallas_call(
        body,
        out_shape=jax.ShapeDtypeStruct((rows, columns), f32),
        grid_spec=pltpu.PrefetchScalarGridSpec(
            num_scalar_prefetch=1,
            grid=(1,),
            in_specs=[VMEM] * (n_stats + 2) + [ANY, ANY],
            out_specs=VMEM,
            scratch_shapes=[
                pltpu.VMEM((rows, width), bf16),
                pltpu.VMEM((2 * width, columns), bf16),
                pltpu.SemaphoreType.DMA((steps,)),
                pltpu.SemaphoreType.DMA,
            ],
        ),
        compiler_params=params(16),
        cost_estimate=cost(4 * rows * width * columns, 4 * width * columns),
        name="query_near",
    )(scalars, *stats, gain, resident(own), in_hbm(other), in_hbm(w_query))


def query_far(half, scalars, stats, gain, near, sources, w_query, cosine, sine):
    rows = sum(piece.shape[0] for piece in sources[0])
    width = sources[0][0].shape[1]
    features, columns = gain.shape[1], w_query.shape[1]
    n_stats, n_pieces = len(stats), len(sources[0])
    held = None if half == 0 else w_query
    total = len(sources) * width
    steps = max(len(sources), STREAMS)
    tile = total // steps
    flat = [piece for source in sources for piece in source]

    def body(scalars_ref, *refs):
        x_refs = refs[n_stats + 2 : n_stats + 2 + len(flat)]
        gain_ref, near_ref = refs[n_stats : n_stats + 2]
        cos_ref, sin_ref, w_ref = refs[n_stats + 2 + len(flat) : n_stats + 5 + len(flat)]
        rest = refs[n_stats + 5 + len(flat) :]
        if held is None:
            out_ref, held_ref, acc_ref, x_held, x_sems, sems = rest
        else:
            out_ref, acc_ref, x_held, x_sems = rest
            held_ref = w_ref
        x_copies = []
        for at, x_ref in enumerate(x_refs):
            piece = x_ref.shape[0]
            first = sum(ref.shape[0] for ref in x_refs[at // n_pieces * n_pieces : at])
            part = x_held.at[at // n_pieces, pl.ds(first, piece), :]
            x_copies.append(pltpu.make_async_copy(x_ref, part, x_sems.at[at]))
            x_copies[at].start()
        places, copies = [], []
        for k in range(steps):
            base = scalars_ref[k * tile // width] * width + k * tile % width
            places.append(pl.ds(pl.multiple_of(base, tile), tile))
            if held is None:
                part = held_ref.at[pl.ds(k * tile, tile), :]
                copies.append(pltpu.make_async_copy(w_ref.at[places[k], :], part, sems.at[k]))
        inverse = inverse_rms(refs[:n_stats], features)
        acc_ref[...] = near_ref[...]
        for k in range(steps):
            first, source = k * tile % width, k * tile // width
            if first == 0:
                for copy in x_copies[source * n_pieces : (source + 1) * n_pieces]:
                    copy.wait()
            piece = x_held[source, :, first : first + tile]
            normed = normalise(piece, inverse, gain_ref[:, places[k]])
            if held is None:
                streamed(copies, k)
            acc_ref[...] += jnp.dot(
                normed, held_ref[k * tile : (k + 1) * tile, :], preferred_element_type=f32
            )
        for head in range(columns // HD):
            part = slice(head * HD, (head + 1) * HD)
            rotated = turn(acc_ref[:, part], cos_ref[...], sin_ref[...])
            out_ref[:, part] = rotated.astype(bf16)

    table = pl.BlockSpec((rows, HD), lambda k, s: (half, 0))
    query = jax.ShapeDtypeStruct((rows, columns), bf16)
    first = held is None
    return pl.pallas_call(
        body,
        out_shape=[query, placed(pltpu.VMEM, (total, columns))] if first else query,
        grid_spec=pltpu.PrefetchScalarGridSpec(
            num_scalar_prefetch=1,
            grid=(1,),
            in_specs=[pl.BlockSpec((8, rows), lambda k, s: (0, half))] * n_stats
            + [VMEM, pl.BlockSpec((rows, columns), lambda k, s: (half, 0))]
            + [ANY] * len(flat)
            + [table, table] + [ANY if first else VMEM],
            out_specs=[VMEM] * 2 if first else VMEM,
            scratch_shapes=[
                pltpu.VMEM((rows, columns), f32),
                pltpu.VMEM((len(sources), rows, width), bf16),
                pltpu.SemaphoreType.DMA((len(flat),)),
            ]
            + [pltpu.SemaphoreType.DMA((steps,))] * first,
        ),
        compiler_params=params(8),
        cost_estimate=cost(2 * rows * total * columns, 2 * total * columns * first),
        name="query_far",
    )(
        scalars, *stats, gain, near, *[in_hbm(x) for x in flat], cosine, sine,
        in_hbm(w_query) if first else resident(held),
    )


def attend_kernel(half, n_rows, pick_ref, q_ref, qdoc_ref, kdoc_ref, *refs):
    *refs, out_ref = refs
    rows, columns = q_ref.shape
    heads = columns // HD
    n_kv = kdoc_ref.shape[1] // refs[0].shape[0]
    kv_refs, mem_refs = refs[:n_kv], refs[n_kv:]
    rows_dev = kv_refs[0].shape[0]
    back = (n_kv - 1) * rows_dev
    low, high = half * rows, back + (half + 1) * rows
    keys, values = [], []
    for at, ref in enumerate(kv_refs):
        first, last = max(low, at * rows_dev), min(high, (at + 1) * rows_dev)
        if first < last:
            part = slice(first - at * rows_dev, last - at * rows_dev)
            keys.append(ref[part, :HD])
            values.append(ref[part, HD:])
    keys, values = jnp.concatenate(keys, 0), jnp.concatenate(values, 0)
    span = high - low
    scale = math.log2(math.e) / math.sqrt(HD)
    blocks = rows // BLK
    for block in range(blocks):
        tokens = slice(block * BLK, (block + 1) * BLK)
        query = jnp.concatenate(
            [q_ref[tokens, h * HD : (h + 1) * HD] for h in range(heads)], 0
        )
        row_index = pick_ref[0]
        number = row_index * (rows_dev // BLK) + half * blocks + block
        server = pick_ref[1 + n_rows + number]
        slot = lax.rem(row_index - server + n_rows, n_rows)
        alive = pick_ref[1 + server]
        mem_keys, mem_values = mem_refs[0][0], mem_refs[0][1]
        for at, ref in enumerate(mem_refs[1:]):
            mem_keys = jnp.where(slot == at + 1, ref[0], mem_keys)
            mem_values = jnp.where(slot == at + 1, ref[1], mem_values)
        column = lax.broadcasted_iota(jnp.int32, (BLK, span), 1)
        row = lax.broadcasted_iota(jnp.int32, (BLK, span), 0)
        mask = (column - back <= row + block * BLK) & (
            kdoc_ref[:, low:high] == qdoc_ref[tokens, :1]
        )
        live = lax.broadcasted_iota(jnp.int32, (1, mem_keys.shape[0]), 1) < alive
        doc = lax.dot_general(query, keys, NT, preferred_element_type=f32)
        mem = lax.dot_general(query, mem_keys, NT, preferred_element_type=f32)
        doc = jnp.where(mask[None], (doc * scale).reshape(heads, BLK, span), masked_score)
        doc = doc.reshape(heads * BLK, span)
        mem = jnp.where(live, mem * scale, masked_score)
        top = jnp.maximum(jnp.max(doc, -1, keepdims=True), jnp.max(mem, -1, keepdims=True))
        doc, mem = jnp.exp2(doc - top), jnp.exp2(mem - top)
        total = jnp.sum(doc, -1, keepdims=True) + jnp.sum(mem, -1, keepdims=True)
        share = 1.0 / total
        mixed = jnp.dot((doc * share).astype(bf16), values, preferred_element_type=f32)
        mixed = mixed + jnp.dot(
            (mem * share).astype(bf16), mem_values, preferred_element_type=f32
        )
        mixed = mixed.astype(bf16)
        for h in range(heads):
            out_ref[tokens, h * HD : (h + 1) * HD] = mixed[h * BLK : (h + 1) * BLK]


def attend_half(half, pick, query, q_doc, k_doc, kv, memories):
    rows, columns = query.shape
    slots = memories[0].shape
    span = k_doc.shape[1] + slots[1]
    return pl.pallas_call(
        functools.partial(attend_kernel, half, len(memories)),
        out_shape=jax.ShapeDtypeStruct(query.shape, bf16),
        grid_spec=pltpu.PrefetchScalarGridSpec(
            num_scalar_prefetch=1,
            grid=(1,),
            in_specs=[
                whole((rows, columns)),
                pl.BlockSpec((rows, HD), lambda i, s: (half, 0)),
                whole(k_doc.shape),
            ]
            + [whole(kv[0].shape)] * len(kv)
            + [whole(slots)] * len(memories),
            out_specs=whole((rows, columns)),
        ),
        compiler_params=params(20),
        cost_estimate=cost(
            4 * rows * columns * span, 4 * rows * columns, rows * columns // HD * span
        ),
        name="attend_half",
    )(pick, query, q_doc, k_doc, *kv, *memories)


def load_columns(scalars, w, width, count):
    parts = 4
    rows = w.shape[0] // parts

    def body(scalars_ref, w_ref, out_ref, sems):
        copies = []
        for k in range(count * parts):
            column = pl.multiple_of(scalars_ref[k // parts] * width, width)
            part = pl.ds(k % parts * rows, rows)
            copies.append(
                pltpu.make_async_copy(
                    w_ref.at[part, pl.ds(column, width)],
                    out_ref.at[part, pl.ds(k // parts * width, width)],
                    sems.at[k],
                )
            )
            copies[k].start()
        for copy in copies:
            copy.wait()

    return pl.pallas_call(
        body,
        out_shape=placed(pltpu.VMEM, (w.shape[0], count * width)),
        grid_spec=pltpu.PrefetchScalarGridSpec(
            num_scalar_prefetch=1,
            grid=(1,),
            in_specs=[ANY],
            out_specs=VMEM,
            scratch_shapes=[pltpu.SemaphoreType.DMA((count * parts,))],
        ),
        compiler_params=params(2),
        cost_estimate=cost(0, 2 * w.shape[0] * count * width),
        name="load_columns",
    )(scalars, in_hbm(w))


def project(attended, held, block, width, sizes, kind=bf16, added=None, begin=0):
    depth = attended[0].shape[1]
    tile = min(width, 512)
    rows = sum(sizes)

    def body(*refs):
        a_refs, w_ref = refs[: len(attended)], refs[len(attended)]
        out_refs = refs[-len(sizes) :]
        for k in range(width // tile):
            part = slice(k * tile, (k + 1) * tile)
            place = slice(block * width + k * tile, block * width + (k + 1) * tile)
            pieces, first = [], 0
            for a_ref in a_refs:
                low, high = max(first, begin), min(first + a_ref.shape[0], begin + rows)
                if low < high:
                    a = a_ref[low - first : high - first, :]
                    pieces.append(jnp.dot(a, w_ref[:, place], preferred_element_type=f32))
                first += a_ref.shape[0]
            total = jnp.concatenate(pieces, 0)
            if added is not None:
                total = total + refs[len(attended) + 1][:, part].astype(f32)
            first = 0
            for size, out_ref in zip(sizes, out_refs):
                out_ref[:, part] = total[first : first + size].astype(kind)
                first += size

    given = [] if added is None else [added]
    return pl.pallas_call(
        body,
        out_shape=[jax.ShapeDtypeStruct((size, width), kind) for size in sizes],
        in_specs=[VMEM] * (len(attended) + 1 + len(given)),
        out_specs=[VMEM] * len(sizes),
        compiler_params=params(8),
        cost_estimate=cost(2 * rows * depth * width, 2 * rows * (depth + width)),
        name="project",
    )(*attended, resident(held), *given)


def on_device(tokens, norm_gain, w_query, w_key, w_value, w_out, doc_ids, assign, res_len, res_mem):
    n_tensor = lax.axis_size("tensor")
    n_rows = lax.axis_size("rows")
    chips = n_tensor // 2
    tensor_index = lax.axis_index("tensor").astype(jnp.int32)
    row_index = lax.axis_index("rows").astype(jnp.int32)
    chip, core = tensor_index // 2, tensor_index % 2
    rows_dev, width = tokens.shape
    features = norm_gain.shape[0]
    kv_heads = w_key.shape[1] // HD
    sharers = n_tensor // kv_heads

    def to_core(x):
        return lax.ppermute(x, "tensor", [(i, i ^ 1) for i in range(n_tensor)])

    def to_chip(x, ahead):
        pairs = [(i, (i + 2 * ahead) % n_tensor) for i in range(n_tensor)]
        return lax.ppermute(x, "tensor", pairs)

    def up(x):
        return lax.ppermute(x, "rows", [(i, (i + 1) % n_rows) for i in range(n_rows)])

    away = range(1, chips)

    half_rows = rows_dev // HALVES
    sizes = [half_rows // 2, half_rows // 2] + [half_rows] * (HALVES - 1)
    *pieces, own_tokens, stat = prep(tokens, sizes)
    chip_stats = [to_chip(stat, ahead) for ahead in away]
    stats = [stat, to_core(stat)] + chip_stats + [to_core(s) for s in chip_stats]

    def gather(piece):
        arrived = [to_chip(piece, ahead) for ahead in away]
        return arrived + [to_core(a) for a in arrived]

    far_pieces = [gather(pieces[0])]
    core_tokens = to_core(tokens)
    near_order = jnp.stack([tensor_index, tensor_index ^ 1])
    far_order = [(tensor_index - 2 * ahead) % n_tensor for ahead in away]
    far_order += [((tensor_index ^ 1) - 2 * ahead) % n_tensor for ahead in away]
    far_order = jnp.stack(far_order)

    head_group = after(tensor_index // sharers, stat)
    memories = [lax.dynamic_slice_in_dim(res_mem[0], head_group * HD, HD, 2)]
    for _ in range(n_rows - 1):
        memories.append(up(memories[-1]))

    half_dim = HD // 2
    lane = jnp.arange(HD, dtype=jnp.int32)
    frequency = rope_base ** (-((lane % half_dim).astype(f32) / half_dim))
    positions = (row_index * rows_dev + jnp.arange(rows_dev, dtype=jnp.int32)).astype(f32)
    angles = positions[:, None] * frequency[None, :]
    cosine = jnp.cos(angles)
    sine = jnp.sin(angles) * jnp.where(lane < half_dim, -1.0, 1.0)[None, :]

    gain = norm_gain.astype(f32)[None]
    targets = jnp.arange(chips, dtype=jnp.int32) * 2
    heads = [(targets + core) // sharers, (targets + 1 - core) // sharers, tensor_index[None]]
    scalars = jnp.concatenate(heads).astype(jnp.int32)
    held = load([after(w_key, stat), w_value])
    scalars = after(scalars, memories[1])
    own, send = kv_partial(scalars, stats, gain, own_tokens, *held, chips)
    arrived = after(to_core(send), *far_pieces[0][: chips - 1])
    pairs = []
    for ahead in away:
        target = (chip + ahead) % chips
        pair = lax.dynamic_index_in_dim(own, target, 0, False).astype(f32)
        pair = pair + lax.dynamic_index_in_dim(arrived, target, 0, False).astype(f32)
        pairs.append(pair.astype(bf16))
    others = [to_chip(pair, ahead) for pair, ahead in zip(pairs, away)]
    for piece in pieces[1:-1]:
        far_pieces.append(gather(after(piece, *pairs)))
    last_piece = after(pieces[-1], *pairs)
    last_arrived = [to_chip(last_piece, ahead) for ahead in away]
    near = query_near(after(near_order, *pairs), stats, gain, own_tokens, core_tokens, w_query)
    kv = [kv_final(own, arrived, others, cosine, sine, after(chip, near, *memories[2:3]))]
    total_rows = n_rows * rows_dev
    longest = total_rows // 2
    back = -(-(longest - 1) // rows_dev)
    targets = []
    for ahead in away:
        far = ((chip + ahead) % chips) * 2
        targets += [far + 1 - core, far + core]
    far_targets = jnp.stack(targets)
    near_targets = jnp.stack([tensor_index ^ 1, tensor_index])
    w_out_far = load_columns(after(far_targets, kv[0]), w_out, width, n_tensor - 2)
    for at in range(back):
        kv.insert(0, up(after(kv[0], w_out_far) if at == 1 else kv[0]))

    padded = jnp.concatenate([jnp.full((back * rows_dev,), -1, jnp.int32), doc_ids])
    k_doc = lax.dynamic_slice_in_dim(padded, row_index * rows_dev, (back + 1) * rows_dev)[None]
    q_doc = jnp.broadcast_to(k_doc[0, back * rows_dev :, None], (rows_dev, HD))
    pick = jnp.concatenate([row_index[None], res_len, assign[:, 0]])

    cuts = [half_rows * 3 // 4, half_rows // 4], [half_rows // 2] * 2
    w_far, ready, attended, outs = w_query, [kv[-1], w_out_far], [], []
    for half in range(HALVES):
        if half == 1:
            arrived = [after(a, attended[0]) for a in last_arrived]
            far_pieces.append(last_arrived + [to_core(a) for a in arrived])
        sources = [list(x) for x in zip(*(far_pieces[:2] if half == 0 else far_pieces[2:]))]
        order = after(far_order, *ready)
        query = query_far(half, order, stats, gain, near, sources, w_far, cosine, sine)
        if half == 0:
            query, w_far = query
        one = attend_half(half, pick, query, q_doc, k_doc, kv, memories)
        attended.append(one)
        one = after(one, *(last_arrived if half == 0 else outs[0]))
        ready, sums = [], [[] for _ in cuts[half]]
        for ahead in away:
            block = 2 * (ahead - 1)
            other = [to_core(x) for x in project([one], w_out_far, block, width, cuts[half])]
            begin = 0
            for at, term in enumerate(other):
                size = cuts[half][at]
                (pair,) = project(
                    [one], w_out_far, block + 1, width, [size], added=term, begin=begin
                )
                begin += size
                ready.append(pair)
                sums[at].append(to_chip(pair, ahead))
        outs += sums
    w_near = load_columns(after(near_targets, *ready), w_out, width, 2)
    w_near = after(w_near, *outs[1], *outs[2])
    (term,) = project(attended, w_near, 0, width, [rows_dev])
    sizes = list(cuts[0]) + list(cuts[1])
    parts = list(project(attended, w_near, 1, width, sizes, f32, to_core(term)))
    for at, arrived in enumerate(outs):
        for piece in arrived:
            parts[at] = parts[at] + piece.astype(f32)
    return jnp.concatenate([part.astype(bf16) for part in parts], 0)


def solution(mesh):
    in_specs = (
        P(("groups", "rows"), "tensor"),
        P(),
        P(None, "tensor"),
        P("tensor", None),
        P("tensor", None),
        P("tensor", None),
        P("groups"),
        P("groups", None),
        P("groups"),
        P(("groups", "rows"), None, None, None),
    )
    out_specs = P(("groups", "rows"), "tensor")
    return jax.shard_map(
        on_device, mesh=mesh, in_specs=in_specs, out_specs=out_specs, check_vma=False
    )
```

```python
import functools
import math

import jax
import jax.numpy as jnp
from jax import lax
from jax.experimental import pallas as pl
from jax.experimental.pallas import tpu as pltpu
from jax.sharding import PartitionSpec as P

HD = 128
BLK = 64
HALVES = 2
STREAMS = 8
CHEAP = 100
DEPTH = 6
SCOPED = 20

norm_eps = 1e-05
rope_base = 500000.0
masked_score = -1e30
MIB = 1 << 20
f32 = jnp.float32
bf16 = jnp.bfloat16
NT = (((1,), (1,)), ((), ()))


def params(mib):
    return pltpu.CompilerParams(vmem_limit_bytes=mib * MIB)


def whole(shape):
    return pl.BlockSpec(shape, lambda *_: (0,) * len(shape))


def resident(x):
    return pltpu.with_memory_space_constraint(x, pltpu.VMEM)


def placed(space, shape, kind=bf16):
    return space(shape, kind)


def in_hbm(x):
    return pltpu.with_memory_space_constraint(x, pltpu.HBM)


VMEM = pl.BlockSpec(memory_space=pltpu.VMEM)
ANY = pl.BlockSpec(memory_space=pl.ANY)


def after(x, *first):
    return lax.optimization_barrier((x, *first))[0]


def cost(flops, moved, exps=0):
    return pl.CostEstimate(
        flops=flops // CHEAP, bytes_accessed=moved // CHEAP, transcendentals=exps // CHEAP
    )


def streamed(copies, at, depth=DEPTH):
    if at == 0:
        for copy in copies[:depth]:
            copy.start()
    copies[at].wait()
    if at + depth < len(copies):
        copies[at + depth].start()


def prep(tokens, sizes):
    rows, width = tokens.shape
    count, parts = len(sizes), 4
    size = rows // parts

    def body(x_ref, *refs):
        *out_refs, held_ref, stat_ref, sems = refs
        firsts = [at * size for at in range(parts)]
        reads = []
        for at, first in enumerate(firsts):
            part = pl.ds(first, size)
            reads.append(
                pltpu.make_async_copy(x_ref.at[part, :], held_ref.at[part, :], sems.at[at])
            )
            reads[at].start()
        begin, copies, totals = 0, [], []
        for at, first in enumerate(firsts):
            reads[at].wait()
            while len(copies) < count and begin + sizes[len(copies)] <= first + size:
                part = pl.ds(begin, sizes[len(copies)])
                sem = sems.at[parts + len(copies)]
                out_ref = out_refs[len(copies)]
                begin += sizes[len(copies)]
                copies.append(pltpu.make_async_copy(held_ref.at[part, :], out_ref, sem))
                copies[-1].start()
            lanes = jnp.zeros((size, HD), f32)
            for k in range(width // HD):
                piece = held_ref[first : first + size, k * HD : (k + 1) * HD].astype(f32)
                lanes = lanes + piece * piece
            totals.append(jnp.sum(lanes, -1, keepdims=True))
        total = jnp.concatenate(totals, 0)
        stat_ref[...] = jnp.broadcast_to(total, (rows, HD)).T[:8, :]
        for copy in copies:
            copy.wait()

    return pl.pallas_call(
        body,
        out_shape=[placed(pltpu.HBM, (piece, width)) for piece in sizes]
        + [placed(pltpu.VMEM, (rows, width)), jax.ShapeDtypeStruct((8, rows), f32)],
        in_specs=[ANY],
        out_specs=[ANY] * count + [VMEM] * 2,
        scratch_shapes=[pltpu.SemaphoreType.DMA((parts + count,))],
        compiler_params=params(SCOPED),
        cost_estimate=cost(2 * rows * width, 4 * rows * width),
        name="prep",
    )(in_hbm(tokens))


def inverse_rms(stat_refs, features):
    total = stat_refs[0][...]
    for ref in stat_refs[1:]:
        total = total + ref[...]
    return lax.rsqrt(total / features + norm_eps).T[:, :1]


def normalise(x, inverse, gain):
    return (x.astype(f32) * inverse * gain).astype(bf16)


def load(arrays):
    def body(*refs):
        count = len(arrays)
        sems = refs[-1]
        copies = [
            pltpu.make_async_copy(refs[at], refs[count + at], sems.at[at]) for at in range(count)
        ]
        for copy in copies:
            copy.start()
        for copy in copies:
            copy.wait()

    moved = sum(a.size * 2 for a in arrays)
    return pl.pallas_call(
        body,
        out_shape=[placed(pltpu.VMEM, a.shape) for a in arrays],
        in_specs=[ANY] * len(arrays),
        out_specs=[VMEM] * len(arrays),
        scratch_shapes=[pltpu.SemaphoreType.DMA((len(arrays),))],
        compiler_params=params(SCOPED),
        cost_estimate=cost(0, moved),
        name="load",
    )(*[in_hbm(a) for a in arrays])


def kv_partial(scalars, stats, gain, tokens, w_key, w_value, chips):
    rows, width = tokens.shape
    features = gain.shape[1]
    kv_width = w_key.shape[1]
    tile = min(width, 512)
    out = jax.ShapeDtypeStruct((chips, rows, 2 * HD), bf16)

    def body(scalars_ref, *refs):
        gain_ref, x_ref, wk_ref, wv_ref, own_ref, send_ref, acc_k, acc_v = refs[len(stats) :]
        inverse = inverse_rms(refs[: len(stats)], features)
        base = scalars_ref[2 * chips] * width
        for k in range(width // tile):
            part = slice(k * tile, (k + 1) * tile)
            gains = gain_ref[:, pl.ds(pl.multiple_of(base + k * tile, tile), tile)]
            normed = normalise(x_ref[:, part], inverse, gains)
            keys = jnp.dot(normed, wk_ref[part, :], preferred_element_type=f32)
            values = jnp.dot(normed, wv_ref[part, :], preferred_element_type=f32)
            acc_k[...] = keys if k == 0 else acc_k[...] + keys
            acc_v[...] = values if k == 0 else acc_v[...] + values
        for at, out_ref in enumerate((own_ref, send_ref)):
            for chip in range(chips):
                head = scalars_ref[at * chips + chip]
                columns = pl.ds(pl.multiple_of(head * HD, HD), HD)
                out_ref[chip, :, :HD] = acc_k[:, columns].astype(bf16)
                out_ref[chip, :, HD:] = acc_v[:, columns].astype(bf16)

    return pl.pallas_call(
        body,
        out_shape=[out, out],
        grid_spec=pltpu.PrefetchScalarGridSpec(
            num_scalar_prefetch=1,
            grid=(1,),
            in_specs=[VMEM] * (len(stats) + 4),
            out_specs=[VMEM] * 2,
            scratch_shapes=[pltpu.VMEM((rows, kv_width), f32)] * 2,
        ),
        compiler_params=params(SCOPED),
        cost_estimate=cost(4 * rows * width * kv_width, 2 * rows * width),
        name="kv_partial",
    )(scalars, *stats, gain, resident(tokens), resident(w_key), resident(w_value))


def turn(x, cosine, sine):
    return x * cosine + pltpu.roll(x, HD // 2, 1) * sine


def kv_final(own, arrived, others, cosine, sine, chip):
    _, rows, width = own.shape

    def body(chip_ref, own_ref, arrived_ref, *refs):
        cos_ref, sin_ref, out_ref = refs[-3:]
        total = own_ref[0].astype(f32) + arrived_ref[0].astype(f32)
        for ref in refs[:-3]:
            total = total + ref[...].astype(f32)
        out_ref[:, :HD] = turn(total[:, :HD], cos_ref[...], sin_ref[...]).astype(bf16)
        out_ref[:, HD:] = total[:, HD:].astype(bf16)

    mine = pl.BlockSpec((1, rows, width), lambda i, s: (s[0], 0, 0))
    return pl.pallas_call(
        body,
        out_shape=jax.ShapeDtypeStruct((rows, width), bf16),
        grid_spec=pltpu.PrefetchScalarGridSpec(
            num_scalar_prefetch=1,
            grid=(1,),
            in_specs=[mine, mine]
            + [whole((rows, width))] * len(others)
            + [whole((rows, HD))] * 2,
            out_specs=whole((rows, width)),
        ),
        compiler_params=params(SCOPED),
        cost_estimate=cost(8 * rows * width, 8 * rows * width),
        name="kv_final",
    )(chip[None], own, arrived, *others, cosine, sine)


def column_copies(columns, w_ref, out_ref, sems, width, parts=4):
    rows = w_ref.shape[0] // parts
    copies = []
    for k in range(len(columns) * parts):
        column = pl.multiple_of(columns[k // parts] * width, width)
        part = pl.ds(k % parts * rows, rows)
        source = w_ref.at[part, pl.ds(column, width)]
        target = out_ref.at[part, pl.ds(k // parts * width, width)]
        copies.append(pltpu.make_async_copy(source, target, sems.at[k]))
    return copies


def load_columns(scalars, w, width, count):
    def body(scalars_ref, w_ref, out_ref, sems):
        columns = [scalars_ref[k] for k in range(count)]
        copies = column_copies(columns, w_ref, out_ref, sems, width)
        for copy in copies:
            copy.start()
        for copy in copies:
            copy.wait()

    return pl.pallas_call(
        body,
        out_shape=placed(pltpu.VMEM, (w.shape[0], count * width)),
        grid_spec=pltpu.PrefetchScalarGridSpec(
            num_scalar_prefetch=1,
            grid=(1,),
            in_specs=[ANY],
            out_specs=VMEM,
            scratch_shapes=[pltpu.SemaphoreType.DMA((count * 4,))],
        ),
        compiler_params=params(SCOPED),
        cost_estimate=cost(0, 2 * w.shape[0] * count * width),
        name="load_columns",
    )(scalars, in_hbm(w))


def query_near(scalars, stats, gain, own, other, w_query):
    rows, width = own.shape
    features, columns = gain.shape[1], w_query.shape[1]
    tile = min(width, 1024)
    steps = 2 * width // tile
    n_stats = len(stats)

    def body(scalars_ref, *refs):
        gain_ref, own_ref, other_ref, w_ref, out_ref, x_held, w_held, sems, x_sem = refs[n_stats:]
        other_copy = pltpu.make_async_copy(other_ref, x_held, x_sem)
        places, copies = [], []
        for k in range(steps):
            base = scalars_ref[k * tile // width] * width + k * tile % width
            places.append(pl.ds(pl.multiple_of(base, tile), tile))
            for part in range(2):
                first = pl.multiple_of(base + part * tile // 2, tile // 2)
                held = w_held.at[pl.ds(k * tile + part * tile // 2, tile // 2), :]
                source = w_ref.at[pl.ds(first, tile // 2), :]
                copies.append(pltpu.make_async_copy(source, held, sems.at[2 * k + part]))
        inverse = None
        for k in range(steps):
            first = k * tile % width
            if k == steps // 2:
                other_copy.wait()
            streamed(copies, 2 * k)
            if k == 0:
                other_copy.start()
                inverse = inverse_rms(refs[:n_stats], features)
            piece = (own_ref if k < steps // 2 else x_held)[:, first : first + tile]
            normed = normalise(piece, inverse, gain_ref[:, places[k]])
            streamed(copies, 2 * k + 1)
            term = jnp.dot(
                normed, w_held[k * tile : (k + 1) * tile, :], preferred_element_type=f32
            )
            out_ref[...] = term if k == 0 else out_ref[...] + term

    return pl.pallas_call(
        body,
        out_shape=placed(pltpu.VMEM, (rows, columns), f32),
        grid_spec=pltpu.PrefetchScalarGridSpec(
            num_scalar_prefetch=1,
            grid=(1,),
            in_specs=[VMEM] * (n_stats + 2) + [ANY, ANY],
            out_specs=VMEM,
            scratch_shapes=[
                pltpu.VMEM((rows, width), bf16),
                pltpu.VMEM((2 * width, columns), bf16),
                pltpu.SemaphoreType.DMA((2 * steps,)),
                pltpu.SemaphoreType.DMA,
            ],
        ),
        compiler_params=params(SCOPED),
        cost_estimate=cost(4 * rows * width * columns, 4 * width * columns),
        name="query_near",
    )(scalars, *stats, gain, resident(own), other, in_hbm(w_query))


def query_far(half, scalars, stats, gain, near, sources, weights, out_width, cosine, sine):
    rows = sum(piece.shape[0] for piece in sources[0])
    width = sources[0][0].shape[1]
    features, columns = gain.shape[1], weights[0].shape[1]
    n_stats, n_pieces = len(stats), len(sources[0])
    total = len(sources) * width
    tile = min(width, 1024)
    steps = total // tile
    flat = [piece for source in sources for piece in source]
    first_half = half == 0

    def body(scalars_ref, *refs):
        x_refs = refs[n_stats + 2 : n_stats + 2 + len(flat)]
        gain_ref, near_ref = refs[n_stats : n_stats + 2]
        cos_ref, sin_ref, w_ref = refs[n_stats + 2 + len(flat) : n_stats + 5 + len(flat)]
        rest = refs[n_stats + 5 + len(flat) :]
        if first_half:
            out_ref, held_ref, acc_ref, x_held, x_sems, sems = rest
        else:
            wo_ref, out_ref, wo_held, acc_ref, x_held, x_sems, sems = rest
            held_ref = w_ref
        x_copies = []
        for at, x_ref in enumerate(x_refs):
            piece = x_ref.shape[0]
            first = sum(ref.shape[0] for ref in x_refs[at // n_pieces * n_pieces : at])
            part = x_held.at[at // n_pieces, pl.ds(first, piece), :]
            x_copies.append(pltpu.make_async_copy(x_ref, part, x_sems.at[at]))
            x_copies[at].start()
        places, copies = [], []
        for k in range(steps):
            base = scalars_ref[k * tile // width] * width + k * tile % width
            places.append(pl.ds(pl.multiple_of(base, tile), tile))
            for part in range(2 * first_half):
                first = pl.multiple_of(base + part * tile // 2, tile // 2)
                held = held_ref.at[pl.ds(k * tile + part * tile // 2, tile // 2), :]
                source = w_ref.at[pl.ds(first, tile // 2), :]
                copies.append(pltpu.make_async_copy(source, held, sems.at[2 * k + part]))
        if not first_half:
            targets = [scalars_ref[len(sources) + k] for k in range(2)]
            copies = column_copies(targets, wo_ref, wo_held, sems, out_width)
            for copy in copies:
                copy.start()
        inverse = None
        for k in range(steps):
            first, source = k * tile % width, k * tile // width
            if first_half:
                streamed(copies, 2 * k)
            if k == 0:
                inverse = inverse_rms(refs[:n_stats], features)
            if first == 0:
                for copy in x_copies[source * n_pieces : (source + 1) * n_pieces]:
                    copy.wait()
            normed = normalise(
                x_held[source, :, first : first + tile], inverse, gain_ref[:, places[k]]
            )
            if first_half:
                streamed(copies, 2 * k + 1)
            term = jnp.dot(
                normed, held_ref[k * tile : (k + 1) * tile, :], preferred_element_type=f32
            )
            given = near_ref[half * rows : (half + 1) * rows, :] if k == 0 else acc_ref[...]
            acc_ref[...] = given + term
        for head in range(columns // HD):
            part = slice(head * HD, (head + 1) * HD)
            rotated = turn(acc_ref[:, part], cos_ref[...], sin_ref[...])
            out_ref[:, part] = rotated.astype(bf16)
        if not first_half:
            for copy in copies:
                copy.wait()

    table = pl.BlockSpec((rows, HD), lambda k, s: (half, 0))
    query = jax.ShapeDtypeStruct((rows, columns), bf16)
    held_shape = (total, columns) if first_half else (columns, 2 * out_width)
    given = [in_hbm(weights[0])] if first_half else [resident(weights[0]), in_hbm(weights[1])]
    return pl.pallas_call(
        body,
        out_shape=[query, placed(pltpu.VMEM, held_shape)],
        grid_spec=pltpu.PrefetchScalarGridSpec(
            num_scalar_prefetch=1,
            grid=(1,),
            in_specs=[pl.BlockSpec((8, rows), lambda k, s: (0, half))] * n_stats
            + [VMEM, VMEM]
            + [ANY] * len(flat)
            + [table, table]
            + ([ANY] if first_half else [VMEM, ANY]),
            out_specs=[VMEM, VMEM],
            scratch_shapes=[
                pltpu.VMEM((rows, columns), f32),
                pltpu.VMEM((len(sources), rows, width), bf16),
                pltpu.SemaphoreType.DMA((len(flat),)),
                pltpu.SemaphoreType.DMA((2 * steps if first_half else 8,)),
            ],
        ),
        compiler_params=params(SCOPED),
        cost_estimate=cost(2 * rows * total * columns, 2 * total * columns),
        name="query_far",
    )(
        scalars, *stats, gain, resident(near), *flat, cosine, sine, *given
    )


def attend_kernel(half, n_rows, pick_ref, q_ref, qdoc_ref, kdoc_ref, *refs):
    *refs, out_ref = refs
    rows, columns = q_ref.shape
    heads = columns // HD
    n_kv = kdoc_ref.shape[1] // refs[0].shape[0]
    kv_refs, mem_refs = refs[:n_kv], refs[n_kv:]
    rows_dev = kv_refs[0].shape[0]
    back = (n_kv - 1) * rows_dev
    low, high = half * rows, back + (half + 1) * rows
    keys, values = [], []
    for at, ref in enumerate(kv_refs):
        first, last = max(low, at * rows_dev), min(high, (at + 1) * rows_dev)
        if first < last:
            part = slice(first - at * rows_dev, last - at * rows_dev)
            keys.append(ref[part, :HD])
            values.append(ref[part, HD:])
    keys, values = jnp.concatenate(keys, 0), jnp.concatenate(values, 0)
    span = high - low
    scale = math.log2(math.e) / math.sqrt(HD)
    blocks = rows // BLK
    for block in range(blocks):
        tokens = slice(block * BLK, (block + 1) * BLK)
        query = jnp.concatenate(
            [q_ref[tokens, h * HD : (h + 1) * HD] for h in range(heads)], 0
        )
        row_index = pick_ref[0]
        number = row_index * (rows_dev // BLK) + half * blocks + block
        server = pick_ref[1 + n_rows + number]
        slot = lax.rem(row_index - server + n_rows, n_rows)
        alive = pick_ref[1 + server]
        mem_keys, mem_values = mem_refs[0][0], mem_refs[0][1]
        for at, ref in enumerate(mem_refs[1:]):
            mem_keys = jnp.where(slot == at + 1, ref[0], mem_keys)
            mem_values = jnp.where(slot == at + 1, ref[1], mem_values)
        column = lax.broadcasted_iota(jnp.int32, (BLK, span), 1)
        row = lax.broadcasted_iota(jnp.int32, (BLK, span), 0)
        mask = (column - back <= row + block * BLK) & (
            kdoc_ref[:, low:high] == qdoc_ref[tokens, :1]
        )
        live = lax.broadcasted_iota(jnp.int32, (1, mem_keys.shape[0]), 1) < alive
        doc = lax.dot_general(query, keys, NT, preferred_element_type=f32)
        mem = lax.dot_general(query, mem_keys, NT, preferred_element_type=f32)
        doc = jnp.where(mask[None], (doc * scale).reshape(heads, BLK, span), masked_score)
        doc = doc.reshape(heads * BLK, span)
        mem = jnp.where(live, mem * scale, masked_score)
        top = jnp.maximum(jnp.max(doc, -1, keepdims=True), jnp.max(mem, -1, keepdims=True))
        doc, mem = jnp.exp2(doc - top), jnp.exp2(mem - top)
        total = jnp.sum(doc, -1, keepdims=True) + jnp.sum(mem, -1, keepdims=True)
        share = 1.0 / total
        mixed = jnp.dot((doc * share).astype(bf16), values, preferred_element_type=f32)
        mixed = mixed + jnp.dot(
            (mem * share).astype(bf16), mem_values, preferred_element_type=f32
        )
        mixed = mixed.astype(bf16)
        for h in range(heads):
            out_ref[tokens, h * HD : (h + 1) * HD] = mixed[h * BLK : (h + 1) * BLK]


def attend_half(half, pick, query, q_doc, k_doc, kv, memories):
    rows, columns = query.shape
    slots = memories[0].shape
    span = k_doc.shape[1] + slots[1]
    return pl.pallas_call(
        functools.partial(attend_kernel, half, len(memories)),
        out_shape=jax.ShapeDtypeStruct(query.shape, bf16),
        grid_spec=pltpu.PrefetchScalarGridSpec(
            num_scalar_prefetch=1,
            grid=(1,),
            in_specs=[
                whole((rows, columns)),
                pl.BlockSpec((rows, HD), lambda i, s: (half, 0)),
                whole(k_doc.shape),
            ]
            + [whole(kv[0].shape)] * len(kv)
            + [whole(slots)] * len(memories),
            out_specs=whole((rows, columns)),
        ),
        compiler_params=params(SCOPED),
        cost_estimate=cost(
            4 * rows * columns * span, 4 * rows * columns, rows * columns // HD * span
        ),
        name="attend_half",
    )(pick, query, q_doc, k_doc, *kv, *memories)


def project(attended, held, block, width, sizes, kind=bf16, added=(), begin=0):
    depth = attended[0].shape[1]
    tile = min(width, 512)
    rows = sum(sizes)

    def body(*refs):
        a_refs, w_ref = refs[: len(attended)], refs[len(attended)]
        out_refs = refs[-len(sizes) :]
        for k in range(width // tile):
            part = slice(k * tile, (k + 1) * tile)
            place = slice(block * width + k * tile, block * width + (k + 1) * tile)
            pieces, first = [], 0
            for a_ref in a_refs:
                low, high = max(first, begin), min(first + a_ref.shape[0], begin + rows)
                if low < high:
                    a = a_ref[low - first : high - first, :]
                    pieces.append(jnp.dot(a, w_ref[:, place], preferred_element_type=f32))
                first += a_ref.shape[0]
            total = jnp.concatenate(pieces, 0)
            if added:
                terms = [ref[:, part].astype(f32) for ref in refs[len(attended) + 1 : -len(sizes)]]
                total = total + jnp.concatenate(terms, 0)
            first = 0
            for size, out_ref in zip(sizes, out_refs):
                out_ref[:, part] = total[first : first + size].astype(kind)
                first += size

    return pl.pallas_call(
        body,
        out_shape=[jax.ShapeDtypeStruct((size, width), kind) for size in sizes],
        in_specs=[VMEM] * (len(attended) + 1 + len(added)),
        out_specs=[VMEM] * len(sizes),
        compiler_params=params(SCOPED),
        cost_estimate=cost(2 * rows * depth * width, 2 * rows * (depth + width)),
        name="project",
    )(*attended, resident(held), *added)


def on_device(tokens, norm_gain, w_query, w_key, w_value, w_out, doc_ids, assign, res_len, res_mem):
    n_tensor = lax.axis_size("tensor")
    n_rows = lax.axis_size("rows")
    chips = n_tensor // 2
    tensor_index = lax.axis_index("tensor").astype(jnp.int32)
    row_index = lax.axis_index("rows").astype(jnp.int32)
    chip, core = tensor_index // 2, tensor_index % 2
    rows_dev, width = tokens.shape
    features = norm_gain.shape[0]
    kv_heads = w_key.shape[1] // HD
    sharers = n_tensor // kv_heads

    def to_core(x):
        return lax.ppermute(x, "tensor", [(i, i ^ 1) for i in range(n_tensor)])

    def to_chip(x, ahead):
        pairs = [(i, (i + 2 * ahead) % n_tensor) for i in range(n_tensor)]
        return lax.ppermute(x, "tensor", pairs)

    def up(x):
        return lax.ppermute(x, "rows", [(i, (i + 1) % n_rows) for i in range(n_rows)])

    away = range(1, chips)

    half_rows = rows_dev // HALVES
    sizes = [half_rows] * HALVES
    *pieces, own_tokens, stat = prep(tokens, sizes)
    chip_stats = [to_chip(stat, ahead) for ahead in away]
    stats = [stat, to_core(stat)] + chip_stats + [to_core(s) for s in chip_stats]

    def gather(piece):
        arrived = [to_chip(piece, ahead) for ahead in away]
        return arrived + [to_core(a) for a in arrived]

    far_pieces = [gather(pieces[0])]
    core_tokens = to_core(tokens)
    near_order = jnp.stack([tensor_index, tensor_index ^ 1])
    far_order = [(tensor_index - 2 * ahead) % n_tensor for ahead in away]
    far_order += [((tensor_index ^ 1) - 2 * ahead) % n_tensor for ahead in away]
    far_order = jnp.stack(far_order)

    head_group = after(tensor_index // sharers, stat)
    memories = [lax.dynamic_slice_in_dim(res_mem[0], head_group * HD, HD, 2)]
    for _ in range(n_rows - 1):
        memories.append(up(memories[-1]))

    half_dim = HD // 2
    lane = jnp.arange(HD, dtype=jnp.int32)
    frequency = rope_base ** (-((lane % half_dim).astype(f32) / half_dim))
    positions = (row_index * rows_dev + jnp.arange(rows_dev, dtype=jnp.int32)).astype(f32)
    angles = positions[:, None] * frequency[None, :]
    cosine = jnp.cos(angles)
    sine = jnp.sin(angles) * jnp.where(lane < half_dim, -1.0, 1.0)[None, :]

    gain = norm_gain.astype(f32)[None]
    targets = jnp.arange(chips, dtype=jnp.int32) * 2
    heads = [(targets + core) // sharers, (targets + 1 - core) // sharers, tensor_index[None]]
    scalars = jnp.concatenate(heads).astype(jnp.int32)
    held = load([after(w_key, stat), w_value])
    own, send = kv_partial(scalars, stats, gain, own_tokens, *held, chips)
    arrived = after(to_core(after(send, memories[1])), *far_pieces[0][: chips - 1])
    pairs = []
    for ahead in away:
        target = (chip + ahead) % chips
        pair = lax.dynamic_index_in_dim(own, target, 0, False).astype(f32)
        pair = pair + lax.dynamic_index_in_dim(arrived, target, 0, False).astype(f32)
        pairs.append(pair.astype(bf16))
    others = [to_chip(pair, ahead) for pair, ahead in zip(pairs, away)]
    targets = []
    for ahead in away:
        far = ((chip + ahead) % chips) * 2
        targets += [far + 1 - core, far + core]
    far_targets = jnp.stack(targets)
    near_targets = jnp.stack([tensor_index ^ 1, tensor_index])
    total_rows = n_rows * rows_dev
    longest = total_rows // 2
    back = -(-(longest - 1) // rows_dev)

    padded = jnp.concatenate([jnp.full((back * rows_dev,), -1, jnp.int32), doc_ids])
    k_doc = lax.dynamic_slice_in_dim(padded, row_index * rows_dev, (back + 1) * rows_dev)[None]
    q_doc = jnp.broadcast_to(k_doc[0, back * rows_dev :, None], (rows_dev, HD))
    pick = jnp.concatenate([row_index[None], res_len, assign[:, 0]])
    far_order = jnp.concatenate([far_order, near_targets])
    small = (k_doc, q_doc, pick, near_order, far_order, cosine, sine)

    w_out_far = load_columns(after(far_targets, *pairs, *small), w_out, width, n_tensor - 2)
    kv = [kv_final(own, arrived, others, cosine, sine, after(chip, w_out_far, *memories[2:3]))]
    last_piece = after(pieces[-1], kv[0])
    last_arrived = [to_chip(last_piece, ahead) for ahead in away]
    near_order = after(near_order, kv[0])
    near = query_near(near_order, stats, gain, own_tokens, core_tokens, w_query)
    for at in range(back):
        kv.insert(0, up(after(kv[0], near) if at == 1 else kv[0]))

    early = half_rows * 3 // 4 // 16 * 16
    cuts = [early, half_rows - early], [half_rows]
    weights, ready, attended, outs = [w_query], [near], [], []
    for half in range(HALVES):
        if half == 1:
            arrived = [after(a, attended[0]) for a in last_arrived]
            far_pieces.append(last_arrived + [to_core(a) for a in arrived])
        sources = [list(x) for x in zip(*(far_pieces[half : half + 1]))]
        order = after(far_order, *ready)
        query, w_held = query_far(
            half, order, stats, gain, near, sources, weights, width, cosine, sine
        )
        weights = [w_held, w_out]
        one = attend_half(half, pick, query, q_doc, k_doc, kv, memories)
        attended.append(one)
        one = after(one, *(last_arrived if half == 0 else outs[0]))
        ready, sums, begin = [], [[] for _ in cuts[half]], 0
        others = []
        for ahead in away:
            block = 2 * (ahead - 1)
            sent = project([one], w_out_far, block, width, cuts[half])
            last = after(attended[-1], *sent)
            others.append([to_core(x) for x in sent])
        if half == HALVES - 1:
            terms = project(attended[:-1] + [last], w_held, 0, width, [rows_dev])
            one = after(one, *terms)
            terms = [to_core(x) for x in terms]
        for at, size in enumerate(cuts[half]):
            for ahead, other in zip(away, others):
                (pair,) = project(
                    [one], w_out_far, 2 * ahead - 1, width, [size], added=[other[at]], begin=begin
                )
                ready.append(pair)
                sums[at].append(to_chip(pair, ahead))
            begin += size
        outs += sums
    sizes = list(cuts[0]) + list(cuts[1])
    own_half = after(attended[-1], *ready)
    parts = list(project([attended[0], own_half], w_held, 1, width, sizes, f32, terms))
    for at, arrived in enumerate(outs):
        for piece in arrived:
            parts[at] = parts[at] + piece.astype(f32)
    return jnp.concatenate([part.astype(bf16) for part in parts], 0)


def solution(mesh):
    in_specs = (
        P(("groups", "rows"), "tensor"),
        P(),
        P(None, "tensor"),
        P("tensor", None),
        P("tensor", None),
        P("tensor", None),
        P("groups"),
        P("groups", None),
        P("groups"),
        P(("groups", "rows"), None, None, None),
    )
    out_specs = P(("groups", "rows"), "tensor")
    return jax.shard_map(
        on_device, mesh=mesh, in_specs=in_specs, out_specs=out_specs, check_vma=False
    )
```

```python
import functools
import math

import jax
import jax.numpy as jnp
from jax import lax
from jax.experimental import pallas as pl
from jax.experimental.pallas import tpu as pltpu
from jax.sharding import PartitionSpec as P

HD = 128
BLK = 64
HALVES = 2
STREAMS = 8
CHEAP = 100
DEPTH = 6
SCOPED = 20

norm_eps = 1e-05
rope_base = 500000.0
masked_score = -1e30
MIB = 1 << 20
f32 = jnp.float32
bf16 = jnp.bfloat16
NT = (((1,), (1,)), ((), ()))


def params(mib):
    return pltpu.CompilerParams(vmem_limit_bytes=mib * MIB)


def whole(shape):
    return pl.BlockSpec(shape, lambda *_: (0,) * len(shape))


def resident(x):
    return pltpu.with_memory_space_constraint(x, pltpu.VMEM)


def placed(space, shape, kind=bf16):
    return space(shape, kind)


def in_hbm(x):
    return pltpu.with_memory_space_constraint(x, pltpu.HBM)


VMEM = pl.BlockSpec(memory_space=pltpu.VMEM)
ANY = pl.BlockSpec(memory_space=pl.ANY)


def after(x, *first):
    return lax.optimization_barrier((x, *first))[0]


def cost(flops, moved, exps=0):
    return pl.CostEstimate(
        flops=flops // CHEAP, bytes_accessed=moved // CHEAP, transcendentals=exps // CHEAP
    )


def streamed(copies, at, depth=DEPTH):
    if at == 0:
        for copy in copies[:depth]:
            copy.start()
    copies[at].wait()
    if at + depth < len(copies):
        copies[at + depth].start()


def prep(tokens, sizes):
    rows, width = tokens.shape
    count, parts = len(sizes), 4
    size = rows // parts

    def body(x_ref, *refs):
        *out_refs, held_ref, stat_ref, sems = refs
        firsts = [at * size for at in range(parts)]
        reads = []
        for at, first in enumerate(firsts):
            part = pl.ds(first, size)
            reads.append(
                pltpu.make_async_copy(x_ref.at[part, :], held_ref.at[part, :], sems.at[at])
            )
            reads[at].start()
        begin, copies, totals = 0, [], []
        for at, first in enumerate(firsts):
            reads[at].wait()
            while len(copies) < count and begin + sizes[len(copies)] <= first + size:
                part = pl.ds(begin, sizes[len(copies)])
                sem = sems.at[parts + len(copies)]
                out_ref = out_refs[len(copies)]
                begin += sizes[len(copies)]
                copies.append(pltpu.make_async_copy(held_ref.at[part, :], out_ref, sem))
                copies[-1].start()
            lanes = jnp.zeros((size, HD), f32)
            for k in range(width // HD):
                piece = held_ref[first : first + size, k * HD : (k + 1) * HD].astype(f32)
                lanes = lanes + piece * piece
            totals.append(jnp.sum(lanes, -1, keepdims=True))
        total = jnp.concatenate(totals, 0)
        stat_ref[...] = jnp.broadcast_to(total, (rows, HD)).T[:8, :]
        for copy in copies:
            copy.wait()

    return pl.pallas_call(
        body,
        out_shape=[placed(pltpu.HBM, (piece, width)) for piece in sizes]
        + [placed(pltpu.VMEM, (rows, width)), jax.ShapeDtypeStruct((8, rows), f32)],
        in_specs=[ANY],
        out_specs=[ANY] * count + [VMEM] * 2,
        scratch_shapes=[pltpu.SemaphoreType.DMA((parts + count,))],
        compiler_params=params(SCOPED),
        cost_estimate=cost(2 * rows * width, 4 * rows * width),
        name="prep",
    )(in_hbm(tokens))


def inverse_rms(stat_refs, features):
    total = stat_refs[0][...]
    for ref in stat_refs[1:]:
        total = total + ref[...]
    return lax.rsqrt(total / features + norm_eps).T[:, :1]


def normalise(x, inverse, gain):
    return (x.astype(f32) * inverse * gain).astype(bf16)


def load(arrays):
    def body(*refs):
        count = len(arrays)
        sems = refs[-1]
        copies = [
            pltpu.make_async_copy(refs[at], refs[count + at], sems.at[at]) for at in range(count)
        ]
        for copy in copies:
            copy.start()
        for copy in copies:
            copy.wait()

    moved = sum(a.size * 2 for a in arrays)
    return pl.pallas_call(
        body,
        out_shape=[placed(pltpu.VMEM, a.shape) for a in arrays],
        in_specs=[ANY] * len(arrays),
        out_specs=[VMEM] * len(arrays),
        scratch_shapes=[pltpu.SemaphoreType.DMA((len(arrays),))],
        compiler_params=params(SCOPED),
        cost_estimate=cost(0, moved),
        name="load",
    )(*[in_hbm(a) for a in arrays])


def kv_partial(scalars, stats, gain, tokens, w_key, w_value, chips):
    rows, width = tokens.shape
    features = gain.shape[1]
    kv_width = w_key.shape[1]
    tile = min(width, 512)
    out = jax.ShapeDtypeStruct((chips, rows, 2 * HD), bf16)

    def body(scalars_ref, *refs):
        gain_ref, x_ref, wk_ref, wv_ref, own_ref, send_ref, acc_k, acc_v = refs[len(stats) :]
        inverse = inverse_rms(refs[: len(stats)], features)
        base = scalars_ref[2 * chips] * width
        for k in range(width // tile):
            part = slice(k * tile, (k + 1) * tile)
            gains = gain_ref[:, pl.ds(pl.multiple_of(base + k * tile, tile), tile)]
            normed = normalise(x_ref[:, part], inverse, gains)
            keys = jnp.dot(normed, wk_ref[part, :], preferred_element_type=f32)
            values = jnp.dot(normed, wv_ref[part, :], preferred_element_type=f32)
            acc_k[...] = keys if k == 0 else acc_k[...] + keys
            acc_v[...] = values if k == 0 else acc_v[...] + values
        for at, out_ref in enumerate((own_ref, send_ref)):
            for chip in range(chips):
                head = scalars_ref[at * chips + chip]
                columns = pl.ds(pl.multiple_of(head * HD, HD), HD)
                out_ref[chip, :, :HD] = acc_k[:, columns].astype(bf16)
                out_ref[chip, :, HD:] = acc_v[:, columns].astype(bf16)

    return pl.pallas_call(
        body,
        out_shape=[out, out],
        grid_spec=pltpu.PrefetchScalarGridSpec(
            num_scalar_prefetch=1,
            grid=(1,),
            in_specs=[VMEM] * (len(stats) + 4),
            out_specs=[VMEM] * 2,
            scratch_shapes=[pltpu.VMEM((rows, kv_width), f32)] * 2,
        ),
        compiler_params=params(SCOPED),
        cost_estimate=cost(4 * rows * width * kv_width, 2 * rows * width),
        name="kv_partial",
    )(scalars, *stats, gain, resident(tokens), resident(w_key), resident(w_value))


def turn(x, cosine, sine):
    return x * cosine + pltpu.roll(x, HD // 2, 1) * sine


def kv_final(own, arrived, others, cosine, sine, chip):
    _, rows, width = own.shape

    def body(chip_ref, own_ref, arrived_ref, *refs):
        cos_ref, sin_ref, out_ref = refs[-3:]
        total = own_ref[0].astype(f32) + arrived_ref[0].astype(f32)
        for ref in refs[:-3]:
            total = total + ref[...].astype(f32)
        out_ref[:, :HD] = turn(total[:, :HD], cos_ref[...], sin_ref[...]).astype(bf16)
        out_ref[:, HD:] = total[:, HD:].astype(bf16)

    mine = pl.BlockSpec((1, rows, width), lambda i, s: (s[0], 0, 0))
    return pl.pallas_call(
        body,
        out_shape=jax.ShapeDtypeStruct((rows, width), bf16),
        grid_spec=pltpu.PrefetchScalarGridSpec(
            num_scalar_prefetch=1,
            grid=(1,),
            in_specs=[mine, mine]
            + [whole((rows, width))] * len(others)
            + [whole((rows, HD))] * 2,
            out_specs=whole((rows, width)),
        ),
        compiler_params=params(SCOPED),
        cost_estimate=cost(8 * rows * width, 8 * rows * width),
        name="kv_final",
    )(chip[None], own, arrived, *others, cosine, sine)


def column_copies(columns, w_ref, out_ref, sems, width, parts=4):
    rows = w_ref.shape[0] // parts
    copies = []
    for k in range(len(columns) * parts):
        column = pl.multiple_of(columns[k // parts] * width, width)
        part = pl.ds(k % parts * rows, rows)
        source = w_ref.at[part, pl.ds(column, width)]
        target = out_ref.at[part, pl.ds(k // parts * width, width)]
        copies.append(pltpu.make_async_copy(source, target, sems.at[k]))
    return copies


def load_columns(scalars, w, width, count):
    def body(scalars_ref, w_ref, out_ref, sems):
        columns = [scalars_ref[k] for k in range(count)]
        copies = column_copies(columns, w_ref, out_ref, sems, width)
        for copy in copies:
            copy.start()
        for copy in copies:
            copy.wait()

    return pl.pallas_call(
        body,
        out_shape=placed(pltpu.VMEM, (w.shape[0], count * width)),
        grid_spec=pltpu.PrefetchScalarGridSpec(
            num_scalar_prefetch=1,
            grid=(1,),
            in_specs=[ANY],
            out_specs=VMEM,
            scratch_shapes=[pltpu.SemaphoreType.DMA((count * 4,))],
        ),
        compiler_params=params(SCOPED),
        cost_estimate=cost(0, 2 * w.shape[0] * count * width),
        name="load_columns",
    )(scalars, in_hbm(w))


def query_near(scalars, stats, gain, own, other, w_query):
    rows, width = own.shape
    features, columns = gain.shape[1], w_query.shape[1]
    tile = min(width, 1024)
    steps = 2 * width // tile
    n_stats = len(stats)

    def body(scalars_ref, *refs):
        gain_ref, own_ref, other_ref, w_ref, out_ref, x_held, w_held, sems, x_sem = refs[n_stats:]
        other_copy = pltpu.make_async_copy(other_ref, x_held, x_sem)
        places, copies = [], []
        for k in range(steps):
            base = scalars_ref[k * tile // width] * width + k * tile % width
            places.append(pl.ds(pl.multiple_of(base, tile), tile))
            for part in range(2):
                first = pl.multiple_of(base + part * tile // 2, tile // 2)
                held = w_held.at[pl.ds(k * tile + part * tile // 2, tile // 2), :]
                source = w_ref.at[pl.ds(first, tile // 2), :]
                copies.append(pltpu.make_async_copy(source, held, sems.at[2 * k + part]))
        inverse = None
        for k in range(steps):
            first = k * tile % width
            if k == steps // 2:
                other_copy.wait()
            streamed(copies, 2 * k)
            if k == 0:
                other_copy.start()
                inverse = inverse_rms(refs[:n_stats], features)
            piece = (own_ref if k < steps // 2 else x_held)[:, first : first + tile]
            normed = normalise(piece, inverse, gain_ref[:, places[k]])
            streamed(copies, 2 * k + 1)
            term = jnp.dot(
                normed, w_held[k * tile : (k + 1) * tile, :], preferred_element_type=f32
            )
            out_ref[...] = term if k == 0 else out_ref[...] + term

    return pl.pallas_call(
        body,
        out_shape=placed(pltpu.VMEM, (rows, columns), f32),
        grid_spec=pltpu.PrefetchScalarGridSpec(
            num_scalar_prefetch=1,
            grid=(1,),
            in_specs=[VMEM] * (n_stats + 2) + [ANY, ANY],
            out_specs=VMEM,
            scratch_shapes=[
                pltpu.VMEM((rows, width), bf16),
                pltpu.VMEM((2 * width, columns), bf16),
                pltpu.SemaphoreType.DMA((2 * steps,)),
                pltpu.SemaphoreType.DMA,
            ],
        ),
        compiler_params=params(SCOPED),
        cost_estimate=cost(4 * rows * width * columns, 4 * width * columns),
        name="query_near",
    )(scalars, *stats, gain, resident(own), other, in_hbm(w_query))


def query_far(half, scalars, stats, gain, near, sources, weights, out_width, cosine, sine):
    rows = sum(piece.shape[0] for piece in sources[0])
    width = sources[0][0].shape[1]
    features, columns = gain.shape[1], weights[0].shape[1]
    n_stats, n_pieces = len(stats), len(sources[0])
    total = len(sources) * width
    tile = min(width, 1024)
    steps = total // tile
    flat = [piece for source in sources for piece in source]
    first_half = half == 0

    def body(scalars_ref, *refs):
        x_refs = refs[n_stats + 2 : n_stats + 2 + len(flat)]
        gain_ref, near_ref = refs[n_stats : n_stats + 2]
        cos_ref, sin_ref, w_ref = refs[n_stats + 2 + len(flat) : n_stats + 5 + len(flat)]
        rest = refs[n_stats + 5 + len(flat) :]
        if first_half:
            out_ref, held_ref, acc_ref, x_held, x_sems, sems = rest
        else:
            wo_ref, out_ref, wo_held, acc_ref, x_held, x_sems, sems = rest
            held_ref = w_ref
        x_copies = []
        for at, x_ref in enumerate(x_refs):
            piece = x_ref.shape[0]
            first = sum(ref.shape[0] for ref in x_refs[at // n_pieces * n_pieces : at])
            part = x_held.at[at // n_pieces, pl.ds(first, piece), :]
            x_copies.append(pltpu.make_async_copy(x_ref, part, x_sems.at[at]))
            x_copies[at].start()
        places, copies = [], []
        for k in range(steps):
            base = scalars_ref[k * tile // width] * width + k * tile % width
            places.append(pl.ds(pl.multiple_of(base, tile), tile))
            for part in range(2 * first_half):
                first = pl.multiple_of(base + part * tile // 2, tile // 2)
                held = held_ref.at[pl.ds(k * tile + part * tile // 2, tile // 2), :]
                source = w_ref.at[pl.ds(first, tile // 2), :]
                copies.append(pltpu.make_async_copy(source, held, sems.at[2 * k + part]))
        if not first_half:
            targets = [scalars_ref[len(sources) + k] for k in range(2)]
            copies = column_copies(targets, wo_ref, wo_held, sems, out_width)
            for copy in copies:
                copy.start()
        inverse = None
        for k in range(steps):
            first, source = k * tile % width, k * tile // width
            if first_half:
                streamed(copies, 2 * k)
            if k == 0:
                inverse = inverse_rms(refs[:n_stats], features)
            if first == 0:
                for copy in x_copies[source * n_pieces : (source + 1) * n_pieces]:
                    copy.wait()
            normed = normalise(
                x_held[source, :, first : first + tile], inverse, gain_ref[:, places[k]]
            )
            if first_half:
                streamed(copies, 2 * k + 1)
            term = jnp.dot(
                normed, held_ref[k * tile : (k + 1) * tile, :], preferred_element_type=f32
            )
            given = near_ref[half * rows : (half + 1) * rows, :] if k == 0 else acc_ref[...]
            acc_ref[...] = given + term
        for head in range(columns // HD):
            part = slice(head * HD, (head + 1) * HD)
            rotated = turn(acc_ref[:, part], cos_ref[...], sin_ref[...])
            out_ref[:, part] = rotated.astype(bf16)
        if not first_half:
            for copy in copies:
                copy.wait()

    table = pl.BlockSpec((rows, HD), lambda k, s: (half, 0))
    query = jax.ShapeDtypeStruct((rows, columns), bf16)
    held_shape = (total, columns) if first_half else (columns, 2 * out_width)
    given = [in_hbm(weights[0])] if first_half else [resident(weights[0]), in_hbm(weights[1])]
    return pl.pallas_call(
        body,
        out_shape=[query, placed(pltpu.VMEM, held_shape)],
        grid_spec=pltpu.PrefetchScalarGridSpec(
            num_scalar_prefetch=1,
            grid=(1,),
            in_specs=[pl.BlockSpec((8, rows), lambda k, s: (0, half))] * n_stats
            + [VMEM, VMEM]
            + [ANY] * len(flat)
            + [table, table]
            + ([ANY] if first_half else [VMEM, ANY]),
            out_specs=[VMEM, VMEM],
            scratch_shapes=[
                pltpu.VMEM((rows, columns), f32),
                pltpu.VMEM((len(sources), rows, width), bf16),
                pltpu.SemaphoreType.DMA((len(flat),)),
                pltpu.SemaphoreType.DMA((2 * steps if first_half else 8,)),
            ],
        ),
        compiler_params=params(SCOPED),
        cost_estimate=cost(2 * rows * total * columns, 2 * total * columns),
        name="query_far",
    )(
        scalars, *stats, gain, resident(near), *flat, cosine, sine, *given
    )


def attend_kernel(half, n_rows, pick_ref, q_ref, qdoc_ref, kdoc_ref, *refs):
    *refs, out_ref = refs
    rows, columns = q_ref.shape
    heads = columns // HD
    n_kv = kdoc_ref.shape[1] // refs[0].shape[0]
    kv_refs, mem_refs = refs[:n_kv], refs[n_kv:]
    rows_dev = kv_refs[0].shape[0]
    back = (n_kv - 1) * rows_dev
    low, high = half * rows, back + (half + 1) * rows
    keys, values = [], []
    for at, ref in enumerate(kv_refs):
        first, last = max(low, at * rows_dev), min(high, (at + 1) * rows_dev)
        if first < last:
            part = slice(first - at * rows_dev, last - at * rows_dev)
            keys.append(ref[part, :HD])
            values.append(ref[part, HD:])
    keys, values = jnp.concatenate(keys, 0), jnp.concatenate(values, 0)
    span = high - low
    scale = math.log2(math.e) / math.sqrt(HD)
    blocks = rows // BLK
    for block in range(blocks):
        tokens = slice(block * BLK, (block + 1) * BLK)
        query = jnp.concatenate(
            [q_ref[tokens, h * HD : (h + 1) * HD] for h in range(heads)], 0
        )
        row_index = pick_ref[0]
        number = row_index * (rows_dev // BLK) + half * blocks + block
        server = pick_ref[1 + n_rows + number]
        slot = lax.rem(row_index - server + n_rows, n_rows)
        alive = pick_ref[1 + server]
        mem_keys, mem_values = mem_refs[0][0], mem_refs[0][1]
        for at, ref in enumerate(mem_refs[1:]):
            mem_keys = jnp.where(slot == at + 1, ref[0], mem_keys)
            mem_values = jnp.where(slot == at + 1, ref[1], mem_values)
        column = lax.broadcasted_iota(jnp.int32, (BLK, span), 1)
        row = lax.broadcasted_iota(jnp.int32, (BLK, span), 0)
        mask = (column - back <= row + block * BLK) & (
            kdoc_ref[:, low:high] == qdoc_ref[tokens, :1]
        )
        live = lax.broadcasted_iota(jnp.int32, (1, mem_keys.shape[0]), 1) < alive
        doc = lax.dot_general(query, keys, NT, preferred_element_type=f32)
        mem = lax.dot_general(query, mem_keys, NT, preferred_element_type=f32)
        doc = jnp.where(mask[None], (doc * scale).reshape(heads, BLK, span), masked_score)
        doc = doc.reshape(heads * BLK, span)
        mem = jnp.where(live, mem * scale, masked_score)
        top = jnp.maximum(jnp.max(doc, -1, keepdims=True), jnp.max(mem, -1, keepdims=True))
        doc, mem = jnp.exp2(doc - top), jnp.exp2(mem - top)
        total = jnp.sum(doc, -1, keepdims=True) + jnp.sum(mem, -1, keepdims=True)
        share = 1.0 / total
        mixed = jnp.dot((doc * share).astype(bf16), values, preferred_element_type=f32)
        mixed = mixed + jnp.dot(
            (mem * share).astype(bf16), mem_values, preferred_element_type=f32
        )
        mixed = mixed.astype(bf16)
        for h in range(heads):
            out_ref[tokens, h * HD : (h + 1) * HD] = mixed[h * BLK : (h + 1) * BLK]


def attend_half(half, pick, query, q_doc, k_doc, kv, memories):
    rows, columns = query.shape
    slots = memories[0].shape
    span = k_doc.shape[1] + slots[1]
    return pl.pallas_call(
        functools.partial(attend_kernel, half, len(memories)),
        out_shape=jax.ShapeDtypeStruct(query.shape, bf16),
        grid_spec=pltpu.PrefetchScalarGridSpec(
            num_scalar_prefetch=1,
            grid=(1,),
            in_specs=[
                whole((rows, columns)),
                pl.BlockSpec((rows, HD), lambda i, s: (half, 0)),
                whole(k_doc.shape),
            ]
            + [whole(kv[0].shape)] * len(kv)
            + [whole(slots)] * len(memories),
            out_specs=whole((rows, columns)),
        ),
        compiler_params=params(SCOPED),
        cost_estimate=cost(
            4 * rows * columns * span, 4 * rows * columns, rows * columns // HD * span
        ),
        name="attend_half",
    )(pick, query, q_doc, k_doc, *kv, *memories)


def project(attended, held, block, width, sizes, kind=bf16, added=(), begin=0, spacer=()):
    depth = attended[0].shape[1]
    tile = min(width, 512)
    rows = sum(sizes)

    def body(*refs):
        a_refs, w_ref = refs[: len(attended)], refs[len(attended)]
        out_refs = refs[-len(sizes) :]
        for k in range(width // tile):
            part = slice(k * tile, (k + 1) * tile)
            place = slice(block * width + k * tile, block * width + (k + 1) * tile)
            pieces, first = [], 0
            for a_ref in a_refs:
                low, high = max(first, begin), min(first + a_ref.shape[0], begin + rows)
                if low < high:
                    a = a_ref[low - first : high - first, :]
                    pieces.append(jnp.dot(a, w_ref[:, place], preferred_element_type=f32))
                first += a_ref.shape[0]
            total = jnp.concatenate(pieces, 0)
            if added:
                terms = [ref[:, part].astype(f32) for ref in refs[len(attended) + 1 :][: len(added)]]
                total = total + jnp.concatenate(terms, 0)
            first = 0
            for size, out_ref in zip(sizes, out_refs):
                out_ref[:, part] = total[first : first + size].astype(kind)
                first += size

    return pl.pallas_call(
        body,
        out_shape=[jax.ShapeDtypeStruct((size, width), kind) for size in sizes],
        in_specs=[VMEM] * (len(attended) + 1 + len(added)) + [ANY] * len(spacer),
        out_specs=[VMEM] * len(sizes),
        compiler_params=params(SCOPED),
        cost_estimate=cost(2 * rows * depth * width, 2 * rows * (depth + width)),
        name="project",
    )(*attended, resident(held), *added, *spacer)


def on_device(tokens, norm_gain, w_query, w_key, w_value, w_out, doc_ids, assign, res_len, res_mem):
    n_tensor = lax.axis_size("tensor")
    n_rows = lax.axis_size("rows")
    chips = n_tensor // 2
    tensor_index = lax.axis_index("tensor").astype(jnp.int32)
    row_index = lax.axis_index("rows").astype(jnp.int32)
    chip, core = tensor_index // 2, tensor_index % 2
    rows_dev, width = tokens.shape
    features = norm_gain.shape[0]
    kv_heads = w_key.shape[1] // HD
    sharers = n_tensor // kv_heads

    def to_core(x):
        return lax.ppermute(x, "tensor", [(i, i ^ 1) for i in range(n_tensor)])

    def to_chip(x, ahead):
        pairs = [(i, (i + 2 * ahead) % n_tensor) for i in range(n_tensor)]
        return lax.ppermute(x, "tensor", pairs)

    def up(x):
        return lax.ppermute(x, "rows", [(i, (i + 1) % n_rows) for i in range(n_rows)])

    away = range(1, chips)

    half_rows = rows_dev // HALVES
    sizes = [half_rows] * HALVES
    *pieces, own_tokens, stat = prep(tokens, sizes)
    chip_stats = [to_chip(stat, ahead) for ahead in away]
    stats = [stat, to_core(stat)] + chip_stats + [to_core(s) for s in chip_stats]

    def gather(piece):
        arrived = [to_chip(piece, ahead) for ahead in away]
        return arrived + [to_core(a) for a in arrived]

    far_pieces = [gather(pieces[0])]
    core_tokens = to_core(tokens)
    near_order = jnp.stack([tensor_index, tensor_index ^ 1])
    far_order = [(tensor_index - 2 * ahead) % n_tensor for ahead in away]
    far_order += [((tensor_index ^ 1) - 2 * ahead) % n_tensor for ahead in away]
    far_order = jnp.stack(far_order)

    head_group = after(tensor_index // sharers, stat)
    memories = [lax.dynamic_slice_in_dim(res_mem[0], head_group * HD, HD, 2)]
    for _ in range(n_rows - 1):
        memories.append(up(memories[-1]))

    half_dim = HD // 2
    lane = jnp.arange(HD, dtype=jnp.int32)
    frequency = rope_base ** (-((lane % half_dim).astype(f32) / half_dim))
    positions = (row_index * rows_dev + jnp.arange(rows_dev, dtype=jnp.int32)).astype(f32)
    angles = positions[:, None] * frequency[None, :]
    cosine = jnp.cos(angles)
    sine = jnp.sin(angles) * jnp.where(lane < half_dim, -1.0, 1.0)[None, :]

    gain = norm_gain.astype(f32)[None]
    targets = jnp.arange(chips, dtype=jnp.int32) * 2
    heads = [(targets + core) // sharers, (targets + 1 - core) // sharers, tensor_index[None]]
    scalars = jnp.concatenate(heads).astype(jnp.int32)
    held = load([after(w_key, stat), w_value])
    own, send = kv_partial(scalars, stats, gain, own_tokens, *held, chips)
    arrived = after(to_core(after(send, memories[1])), *far_pieces[0][: chips - 1])
    pairs = []
    for ahead in away:
        target = (chip + ahead) % chips
        pair = lax.dynamic_index_in_dim(own, target, 0, False).astype(f32)
        pair = pair + lax.dynamic_index_in_dim(arrived, target, 0, False).astype(f32)
        pairs.append(pair.astype(bf16))
    others = [to_chip(pair, ahead) for pair, ahead in zip(pairs, away)]
    targets = []
    for ahead in away:
        far = ((chip + ahead) % chips) * 2
        targets += [far + 1 - core, far + core]
    far_targets = jnp.stack(targets)
    near_targets = jnp.stack([tensor_index ^ 1, tensor_index])
    total_rows = n_rows * rows_dev
    longest = total_rows // 2
    back = -(-(longest - 1) // rows_dev)

    padded = jnp.concatenate([jnp.full((back * rows_dev,), -1, jnp.int32), doc_ids])
    k_doc = lax.dynamic_slice_in_dim(padded, row_index * rows_dev, (back + 1) * rows_dev)[None]
    q_doc = jnp.broadcast_to(k_doc[0, back * rows_dev :, None], (rows_dev, HD))
    pick = jnp.concatenate([row_index[None], res_len, assign[:, 0]])
    far_order = jnp.concatenate([far_order, near_targets])
    small = (k_doc, q_doc, pick, near_order, far_order, cosine, sine)

    w_out_far = load_columns(after(far_targets, *pairs, *small), w_out, width, n_tensor - 2)
    kv = [kv_final(own, arrived, others, cosine, sine, after(chip, w_out_far, *memories[2:3]))]
    last_piece = after(pieces[-1], kv[0])
    last_arrived = [to_chip(last_piece, ahead) for ahead in away]
    near_order = after(near_order, kv[0])
    near = query_near(near_order, stats, gain, own_tokens, core_tokens, w_query)
    for at in range(back):
        kv.insert(0, up(after(kv[0], near) if at == 1 else kv[0]))

    cuts = [half_rows], [half_rows]
    weights, ready, attended, outs = [w_query], [near], [], []
    for half in range(HALVES):
        if half == 1:
            arrived = [after(a, attended[0]) for a in last_arrived]
            far_pieces.append(last_arrived + [to_core(a) for a in arrived])
        sources = [list(x) for x in zip(*(far_pieces[half : half + 1]))]
        order = after(far_order, *ready)
        query, w_held = query_far(
            half, order, stats, gain, near, sources, weights, width, cosine, sine
        )
        weights = [w_held, w_out]
        one = attend_half(half, pick, query, q_doc, k_doc, kv, memories)
        attended.append(one)
        one = after(one, *(last_arrived if half == 0 else ()))
        ready, sums, begin = [], [[] for _ in cuts[half]], 0
        others, spacer = [], []
        for ahead in away:
            block = 2 * (ahead - 1)
            sent = project([one], w_out_far, block, width, cuts[half])
            last = after(attended[-1], *sent)
            others.append([to_core(x) for x in sent])
        if half == HALVES - 1:
            terms = project(attended[:-1] + [last], w_held, 0, width, [half_rows // 2] * (2 * HALVES))
            one = after(one, *terms)
            spacer = [to_core(after(memories[0], *outs[0], *terms))]
            terms = [to_core(x) for x in terms]
        for at, size in enumerate(cuts[half]):
            for ahead, other in zip(away, others):
                (pair,) = project(
                    [one], w_out_far, 2 * ahead - 1, width, [size], added=[other[at]], begin=begin,
                    spacer=spacer,
                )
                ready.append(pair)
                sums[at].append(to_chip(pair, ahead))
            begin += size
        outs += sums
    sizes = list(cuts[0]) + list(cuts[1])
    own_half = after(attended[-1], *ready)
    parts = list(project([attended[0], own_half], w_held, 1, width, sizes, f32, terms))
    for at, arrived in enumerate(outs):
        for piece in arrived:
            parts[at] = parts[at] + piece.astype(f32)
    return jnp.concatenate([part.astype(bf16) for part in parts], 0)


def solution(mesh):
    in_specs = (
        P(("groups", "rows"), "tensor"),
        P(),
        P(None, "tensor"),
        P("tensor", None),
        P("tensor", None),
        P("tensor", None),
        P("groups"),
        P("groups", None),
        P("groups"),
        P(("groups", "rows"), None, None, None),
    )
    out_specs = P(("groups", "rows"), "tensor")
    return jax.shard_map(
        on_device, mesh=mesh, in_specs=in_specs, out_specs=out_specs, check_vma=False
    )
```

```python
import functools
import math

import jax
import jax.numpy as jnp
from jax import lax
from jax.experimental import pallas as pl
from jax.experimental.pallas import tpu as pltpu
from jax.sharding import PartitionSpec as P

HD = 128
BLK = 64
HALVES = 2
STREAMS = 8
CHEAP = 100
DEPTH = 6
SCOPED = 20

norm_eps = 1e-05
rope_base = 500000.0
masked_score = -1e30
MIB = 1 << 20
f32 = jnp.float32
bf16 = jnp.bfloat16
NT = (((1,), (1,)), ((), ()))


def params(mib):
    return pltpu.CompilerParams(vmem_limit_bytes=mib * MIB)


def whole(shape):
    return pl.BlockSpec(shape, lambda *_: (0,) * len(shape))


def resident(x):
    return pltpu.with_memory_space_constraint(x, pltpu.VMEM)


def placed(space, shape, kind=bf16):
    return space(shape, kind)


def in_hbm(x):
    return pltpu.with_memory_space_constraint(x, pltpu.HBM)


VMEM = pl.BlockSpec(memory_space=pltpu.VMEM)
ANY = pl.BlockSpec(memory_space=pl.ANY)


def after(x, *first):
    return lax.optimization_barrier((x, *first))[0]


def cost(flops, moved, exps=0):
    return pl.CostEstimate(
        flops=flops // CHEAP, bytes_accessed=moved // CHEAP, transcendentals=exps // CHEAP
    )


def streamed(copies, at, depth=DEPTH):
    if at == 0:
        for copy in copies[:depth]:
            copy.start()
    copies[at].wait()
    if at + depth < len(copies):
        copies[at + depth].start()


def prep(tokens, sizes):
    rows, width = tokens.shape
    count, parts = len(sizes), 4
    size = rows // parts

    def body(x_ref, *refs):
        *out_refs, held_ref, stat_ref, sems = refs
        firsts = [at * size for at in range(parts)]
        reads = []
        for at, first in enumerate(firsts):
            part = pl.ds(first, size)
            reads.append(
                pltpu.make_async_copy(x_ref.at[part, :], held_ref.at[part, :], sems.at[at])
            )
            reads[at].start()
        begin, copies, totals = 0, [], []
        for at, first in enumerate(firsts):
            reads[at].wait()
            while len(copies) < count and begin + sizes[len(copies)] <= first + size:
                part = pl.ds(begin, sizes[len(copies)])
                sem = sems.at[parts + len(copies)]
                out_ref = out_refs[len(copies)]
                begin += sizes[len(copies)]
                copies.append(pltpu.make_async_copy(held_ref.at[part, :], out_ref, sem))
                copies[-1].start()
            lanes = jnp.zeros((size, HD), f32)
            for k in range(width // HD):
                piece = held_ref[first : first + size, k * HD : (k + 1) * HD].astype(f32)
                lanes = lanes + piece * piece
            totals.append(jnp.sum(lanes, -1, keepdims=True))
        total = jnp.concatenate(totals, 0)
        stat_ref[...] = jnp.broadcast_to(total, (rows, HD)).T[:8, :]
        for copy in copies:
            copy.wait()

    return pl.pallas_call(
        body,
        out_shape=[placed(pltpu.HBM, (piece, width)) for piece in sizes]
        + [placed(pltpu.VMEM, (rows, width)), jax.ShapeDtypeStruct((8, rows), f32)],
        in_specs=[ANY],
        out_specs=[ANY] * count + [VMEM] * 2,
        scratch_shapes=[pltpu.SemaphoreType.DMA((parts + count,))],
        compiler_params=params(SCOPED),
        cost_estimate=cost(2 * rows * width, 4 * rows * width),
        name="prep",
    )(in_hbm(tokens))


def inverse_rms(stat_refs, features):
    total = stat_refs[0][...]
    for ref in stat_refs[1:]:
        total = total + ref[...]
    return lax.rsqrt(total / features + norm_eps).T[:, :1]


def normalise(x, inverse, gain):
    return (x.astype(f32) * inverse * gain).astype(bf16)


def load(arrays):
    def body(*refs):
        count = len(arrays)
        sems = refs[-1]
        copies = [
            pltpu.make_async_copy(refs[at], refs[count + at], sems.at[at]) for at in range(count)
        ]
        for copy in copies:
            copy.start()
        for copy in copies:
            copy.wait()

    moved = sum(a.size * 2 for a in arrays)
    return pl.pallas_call(
        body,
        out_shape=[placed(pltpu.VMEM, a.shape) for a in arrays],
        in_specs=[ANY] * len(arrays),
        out_specs=[VMEM] * len(arrays),
        scratch_shapes=[pltpu.SemaphoreType.DMA((len(arrays),))],
        compiler_params=params(SCOPED),
        cost_estimate=cost(0, moved),
        name="load",
    )(*[in_hbm(a) for a in arrays])


def kv_partial(scalars, stats, gain, tokens, w_key, w_value, chips):
    rows, width = tokens.shape
    features = gain.shape[1]
    kv_width = w_key.shape[1]
    tile = min(width, 512)
    out = jax.ShapeDtypeStruct((chips, rows, 2 * HD), bf16)

    def body(scalars_ref, *refs):
        gain_ref, x_ref, wk_ref, wv_ref, own_ref, send_ref, acc_k, acc_v = refs[len(stats) :]
        inverse = inverse_rms(refs[: len(stats)], features)
        base = scalars_ref[2 * chips] * width
        for k in range(width // tile):
            part = slice(k * tile, (k + 1) * tile)
            gains = gain_ref[:, pl.ds(pl.multiple_of(base + k * tile, tile), tile)]
            normed = normalise(x_ref[:, part], inverse, gains)
            keys = jnp.dot(normed, wk_ref[part, :], preferred_element_type=f32)
            values = jnp.dot(normed, wv_ref[part, :], preferred_element_type=f32)
            acc_k[...] = keys if k == 0 else acc_k[...] + keys
            acc_v[...] = values if k == 0 else acc_v[...] + values
        for at, out_ref in enumerate((own_ref, send_ref)):
            for chip in range(chips):
                head = scalars_ref[at * chips + chip]
                columns = pl.ds(pl.multiple_of(head * HD, HD), HD)
                out_ref[chip, :, :HD] = acc_k[:, columns].astype(bf16)
                out_ref[chip, :, HD:] = acc_v[:, columns].astype(bf16)

    return pl.pallas_call(
        body,
        out_shape=[out, out],
        grid_spec=pltpu.PrefetchScalarGridSpec(
            num_scalar_prefetch=1,
            grid=(1,),
            in_specs=[VMEM] * (len(stats) + 4),
            out_specs=[VMEM] * 2,
            scratch_shapes=[pltpu.VMEM((rows, kv_width), f32)] * 2,
        ),
        compiler_params=params(SCOPED),
        cost_estimate=cost(4 * rows * width * kv_width, 2 * rows * width),
        name="kv_partial",
    )(scalars, *stats, gain, resident(tokens), resident(w_key), resident(w_value))


def turn(x, cosine, sine):
    return x * cosine + pltpu.roll(x, HD // 2, 1) * sine


def kv_final(own, arrived, others, cosine, sine, chip):
    _, rows, width = own.shape

    def body(chip_ref, own_ref, arrived_ref, *refs):
        cos_ref, sin_ref, out_ref = refs[-3:]
        total = own_ref[0].astype(f32) + arrived_ref[0].astype(f32)
        for ref in refs[:-3]:
            total = total + ref[...].astype(f32)
        out_ref[:, :HD] = turn(total[:, :HD], cos_ref[...], sin_ref[...]).astype(bf16)
        out_ref[:, HD:] = total[:, HD:].astype(bf16)

    mine = pl.BlockSpec((1, rows, width), lambda i, s: (s[0], 0, 0))
    return pl.pallas_call(
        body,
        out_shape=jax.ShapeDtypeStruct((rows, width), bf16),
        grid_spec=pltpu.PrefetchScalarGridSpec(
            num_scalar_prefetch=1,
            grid=(1,),
            in_specs=[mine, mine]
            + [whole((rows, width))] * len(others)
            + [whole((rows, HD))] * 2,
            out_specs=whole((rows, width)),
        ),
        compiler_params=params(SCOPED),
        cost_estimate=cost(8 * rows * width, 8 * rows * width),
        name="kv_final",
    )(chip[None], own, arrived, *others, cosine, sine)


def column_copies(columns, w_ref, out_ref, sems, width, parts=4):
    rows = w_ref.shape[0] // parts
    copies = []
    for k in range(len(columns) * parts):
        column = pl.multiple_of(columns[k // parts] * width, width)
        part = pl.ds(k % parts * rows, rows)
        source = w_ref.at[part, pl.ds(column, width)]
        target = out_ref.at[part, pl.ds(k // parts * width, width)]
        copies.append(pltpu.make_async_copy(source, target, sems.at[k]))
    return copies


def load_columns(scalars, w, width, count):
    def body(scalars_ref, w_ref, out_ref, sems):
        columns = [scalars_ref[k] for k in range(count)]
        copies = column_copies(columns, w_ref, out_ref, sems, width)
        for copy in copies:
            copy.start()
        for copy in copies:
            copy.wait()

    return pl.pallas_call(
        body,
        out_shape=placed(pltpu.VMEM, (w.shape[0], count * width)),
        grid_spec=pltpu.PrefetchScalarGridSpec(
            num_scalar_prefetch=1,
            grid=(1,),
            in_specs=[ANY],
            out_specs=VMEM,
            scratch_shapes=[pltpu.SemaphoreType.DMA((count * 4,))],
        ),
        compiler_params=params(SCOPED),
        cost_estimate=cost(0, 2 * w.shape[0] * count * width),
        name="load_columns",
    )(scalars, in_hbm(w))


def query_near(scalars, stats, gain, own, other, w_query):
    rows, width = own.shape
    features, columns = gain.shape[1], w_query.shape[1]
    tile = min(width, 1024)
    steps = 2 * width // tile
    n_stats = len(stats)

    def body(scalars_ref, *refs):
        gain_ref, own_ref, other_ref, w_ref, out_ref, x_held, w_held, sems, x_sem = refs[n_stats:]
        other_copy = pltpu.make_async_copy(other_ref, x_held, x_sem)
        places, copies = [], []
        for k in range(steps):
            base = scalars_ref[k * tile // width] * width + k * tile % width
            places.append(pl.ds(pl.multiple_of(base, tile), tile))
            for part in range(2):
                first = pl.multiple_of(base + part * tile // 2, tile // 2)
                held = w_held.at[pl.ds(k * tile + part * tile // 2, tile // 2), :]
                source = w_ref.at[pl.ds(first, tile // 2), :]
                copies.append(pltpu.make_async_copy(source, held, sems.at[2 * k + part]))
        inverse = None
        for k in range(steps):
            first = k * tile % width
            if k == steps // 2:
                other_copy.wait()
            streamed(copies, 2 * k)
            if k == 0:
                other_copy.start()
                inverse = inverse_rms(refs[:n_stats], features)
            piece = (own_ref if k < steps // 2 else x_held)[:, first : first + tile]
            normed = normalise(piece, inverse, gain_ref[:, places[k]])
            streamed(copies, 2 * k + 1)
            term = jnp.dot(
                normed, w_held[k * tile : (k + 1) * tile, :], preferred_element_type=f32
            )
            out_ref[...] = term if k == 0 else out_ref[...] + term

    return pl.pallas_call(
        body,
        out_shape=placed(pltpu.VMEM, (rows, columns), f32),
        grid_spec=pltpu.PrefetchScalarGridSpec(
            num_scalar_prefetch=1,
            grid=(1,),
            in_specs=[VMEM] * (n_stats + 2) + [ANY, ANY],
            out_specs=VMEM,
            scratch_shapes=[
                pltpu.VMEM((rows, width), bf16),
                pltpu.VMEM((2 * width, columns), bf16),
                pltpu.SemaphoreType.DMA((2 * steps,)),
                pltpu.SemaphoreType.DMA,
            ],
        ),
        compiler_params=params(SCOPED),
        cost_estimate=cost(4 * rows * width * columns, 4 * width * columns),
        name="query_near",
    )(scalars, *stats, gain, resident(own), other, in_hbm(w_query))


def query_far(half, scalars, stats, gain, near, sources, weights, out_width, cosine, sine):
    rows = sum(piece.shape[0] for piece in sources[0])
    width = sources[0][0].shape[1]
    features, columns = gain.shape[1], weights[0].shape[1]
    n_stats, n_pieces = len(stats), len(sources[0])
    total = len(sources) * width
    tile = min(width, 1024)
    steps = total // tile
    flat = [piece for source in sources for piece in source]
    first_half = half == 0

    def body(scalars_ref, *refs):
        x_refs = refs[n_stats + 2 : n_stats + 2 + len(flat)]
        gain_ref, near_ref = refs[n_stats : n_stats + 2]
        cos_ref, sin_ref, w_ref = refs[n_stats + 2 + len(flat) : n_stats + 5 + len(flat)]
        rest = refs[n_stats + 5 + len(flat) :]
        if first_half:
            out_ref, held_ref, acc_ref, x_held, x_sems, sems = rest
        else:
            wo_ref, out_ref, wo_held, acc_ref, x_held, x_sems, sems = rest
            held_ref = w_ref
        x_copies = []
        for at, x_ref in enumerate(x_refs):
            piece = x_ref.shape[0]
            first = sum(ref.shape[0] for ref in x_refs[at // n_pieces * n_pieces : at])
            part = x_held.at[at // n_pieces, pl.ds(first, piece), :]
            x_copies.append(pltpu.make_async_copy(x_ref, part, x_sems.at[at]))
            x_copies[at].start()
        places, copies = [], []
        for k in range(steps):
            base = scalars_ref[k * tile // width] * width + k * tile % width
            places.append(pl.ds(pl.multiple_of(base, tile), tile))
            for part in range(2 * first_half):
                first = pl.multiple_of(base + part * tile // 2, tile // 2)
                held = held_ref.at[pl.ds(k * tile + part * tile // 2, tile // 2), :]
                source = w_ref.at[pl.ds(first, tile // 2), :]
                copies.append(pltpu.make_async_copy(source, held, sems.at[2 * k + part]))
        if not first_half:
            targets = [scalars_ref[len(sources) + k] for k in range(2)]
            copies = column_copies(targets, wo_ref, wo_held, sems, out_width)
            for copy in copies:
                copy.start()
        inverse = None
        for k in range(steps):
            first, source = k * tile % width, k * tile // width
            if first_half:
                streamed(copies, 2 * k)
            if k == 0:
                inverse = inverse_rms(refs[:n_stats], features)
            if first == 0:
                for copy in x_copies[source * n_pieces : (source + 1) * n_pieces]:
                    copy.wait()
            normed = normalise(
                x_held[source, :, first : first + tile], inverse, gain_ref[:, places[k]]
            )
            if first_half:
                streamed(copies, 2 * k + 1)
            term = jnp.dot(
                normed, held_ref[k * tile : (k + 1) * tile, :], preferred_element_type=f32
            )
            given = near_ref[half * rows : (half + 1) * rows, :] if k == 0 else acc_ref[...]
            acc_ref[...] = given + term
        for head in range(columns // HD):
            part = slice(head * HD, (head + 1) * HD)
            rotated = turn(acc_ref[:, part], cos_ref[...], sin_ref[...])
            out_ref[:, part] = rotated.astype(bf16)
        if not first_half:
            for copy in copies:
                copy.wait()

    table = pl.BlockSpec((rows, HD), lambda k, s: (half, 0))
    query = jax.ShapeDtypeStruct((rows, columns), bf16)
    held_shape = (total, columns) if first_half else (columns, 2 * out_width)
    given = [in_hbm(weights[0])] if first_half else [resident(weights[0]), in_hbm(weights[1])]
    return pl.pallas_call(
        body,
        out_shape=[query, placed(pltpu.VMEM, held_shape)],
        grid_spec=pltpu.PrefetchScalarGridSpec(
            num_scalar_prefetch=1,
            grid=(1,),
            in_specs=[pl.BlockSpec((8, rows), lambda k, s: (0, half))] * n_stats
            + [VMEM, VMEM]
            + [ANY] * len(flat)
            + [table, table]
            + ([ANY] if first_half else [VMEM, ANY]),
            out_specs=[VMEM, VMEM],
            scratch_shapes=[
                pltpu.VMEM((rows, columns), f32),
                pltpu.VMEM((len(sources), rows, width), bf16),
                pltpu.SemaphoreType.DMA((len(flat),)),
                pltpu.SemaphoreType.DMA((2 * steps if first_half else 8,)),
            ],
        ),
        compiler_params=params(SCOPED),
        cost_estimate=cost(2 * rows * total * columns, 2 * total * columns),
        name="query_far",
    )(
        scalars, *stats, gain, resident(near), *flat, cosine, sine, *given
    )


def attend_kernel(half, n_rows, pick_ref, q_ref, qdoc_ref, kdoc_ref, *refs):
    *refs, out_ref = refs
    rows, columns = q_ref.shape
    heads = columns // HD
    n_kv = kdoc_ref.shape[1] // refs[0].shape[0]
    kv_refs, mem_refs = refs[:n_kv], refs[n_kv:]
    rows_dev = kv_refs[0].shape[0]
    back = (n_kv - 1) * rows_dev
    low, high = half * rows, back + (half + 1) * rows
    keys, values = [], []
    for at, ref in enumerate(kv_refs):
        first, last = max(low, at * rows_dev), min(high, (at + 1) * rows_dev)
        if first < last:
            part = slice(first - at * rows_dev, last - at * rows_dev)
            keys.append(ref[part, :HD])
            values.append(ref[part, HD:])
    keys, values = jnp.concatenate(keys, 0), jnp.concatenate(values, 0)
    span = high - low
    scale = math.log2(math.e) / math.sqrt(HD)
    blocks = rows // BLK
    for block in range(blocks):
        tokens = slice(block * BLK, (block + 1) * BLK)
        query = jnp.concatenate(
            [q_ref[tokens, h * HD : (h + 1) * HD] for h in range(heads)], 0
        )
        row_index = pick_ref[0]
        number = row_index * (rows_dev // BLK) + half * blocks + block
        server = pick_ref[1 + n_rows + number]
        slot = lax.rem(row_index - server + n_rows, n_rows)
        alive = pick_ref[1 + server]
        mem_keys, mem_values = mem_refs[0][0], mem_refs[0][1]
        for at, ref in enumerate(mem_refs[1:]):
            mem_keys = jnp.where(slot == at + 1, ref[0], mem_keys)
            mem_values = jnp.where(slot == at + 1, ref[1], mem_values)
        column = lax.broadcasted_iota(jnp.int32, (BLK, span), 1)
        row = lax.broadcasted_iota(jnp.int32, (BLK, span), 0)
        mask = (column - back <= row + block * BLK) & (
            kdoc_ref[:, low:high] == qdoc_ref[tokens, :1]
        )
        live = lax.broadcasted_iota(jnp.int32, (1, mem_keys.shape[0]), 1) < alive
        doc = lax.dot_general(query, keys, NT, preferred_element_type=f32)
        mem = lax.dot_general(query, mem_keys, NT, preferred_element_type=f32)
        doc = jnp.where(mask[None], (doc * scale).reshape(heads, BLK, span), masked_score)
        doc = doc.reshape(heads * BLK, span)
        mem = jnp.where(live, mem * scale, masked_score)
        top = jnp.maximum(jnp.max(doc, -1, keepdims=True), jnp.max(mem, -1, keepdims=True))
        doc, mem = jnp.exp2(doc - top), jnp.exp2(mem - top)
        total = jnp.sum(doc, -1, keepdims=True) + jnp.sum(mem, -1, keepdims=True)
        share = 1.0 / total
        mixed = jnp.dot((doc * share).astype(bf16), values, preferred_element_type=f32)
        mixed = mixed + jnp.dot(
            (mem * share).astype(bf16), mem_values, preferred_element_type=f32
        )
        mixed = mixed.astype(bf16)
        for h in range(heads):
            out_ref[tokens, h * HD : (h + 1) * HD] = mixed[h * BLK : (h + 1) * BLK]


def attend_half(half, pick, query, q_doc, k_doc, kv, memories):
    rows, columns = query.shape
    slots = memories[0].shape
    span = k_doc.shape[1] + slots[1]
    return pl.pallas_call(
        functools.partial(attend_kernel, half, len(memories)),
        out_shape=jax.ShapeDtypeStruct(query.shape, bf16),
        grid_spec=pltpu.PrefetchScalarGridSpec(
            num_scalar_prefetch=1,
            grid=(1,),
            in_specs=[
                whole((rows, columns)),
                pl.BlockSpec((rows, HD), lambda i, s: (half, 0)),
                whole(k_doc.shape),
            ]
            + [whole(kv[0].shape)] * len(kv)
            + [whole(slots)] * len(memories),
            out_specs=whole((rows, columns)),
        ),
        compiler_params=params(SCOPED),
        cost_estimate=cost(
            4 * rows * columns * span, 4 * rows * columns, rows * columns // HD * span
        ),
        name="attend_half",
    )(pick, query, q_doc, k_doc, *kv, *memories)


def project(attended, held, block, width, sizes, kind=bf16, added=(), begin=0, spacer=()):
    depth = attended[0].shape[1]
    tile = min(width, 512)
    rows = sum(sizes)

    def body(*refs):
        a_refs, w_ref = refs[: len(attended)], refs[len(attended)]
        out_refs = refs[-len(sizes) :]
        for k in range(width // tile):
            part = slice(k * tile, (k + 1) * tile)
            place = slice(block * width + k * tile, block * width + (k + 1) * tile)
            pieces, first = [], 0
            for a_ref in a_refs:
                low, high = max(first, begin), min(first + a_ref.shape[0], begin + rows)
                if low < high:
                    a = a_ref[low - first : high - first, :]
                    pieces.append(jnp.dot(a, w_ref[:, place], preferred_element_type=f32))
                first += a_ref.shape[0]
            total = jnp.concatenate(pieces, 0)
            if added:
                terms = [ref[:, part].astype(f32) for ref in refs[len(attended) + 1 :][: len(added)]]
                total = total + jnp.concatenate(terms, 0)
            first = 0
            for size, out_ref in zip(sizes, out_refs):
                out_ref[:, part] = total[first : first + size].astype(kind)
                first += size

    return pl.pallas_call(
        body,
        out_shape=[jax.ShapeDtypeStruct((size, width), kind) for size in sizes],
        in_specs=[VMEM] * (len(attended) + 1 + len(added)) + [ANY] * len(spacer),
        out_specs=[VMEM] * len(sizes),
        compiler_params=params(SCOPED),
        cost_estimate=cost(2 * rows * depth * width, 2 * rows * (depth + width)),
        name="project",
    )(*attended, resident(held), *added, *spacer)


def on_device(tokens, norm_gain, w_query, w_key, w_value, w_out, doc_ids, assign, res_len, res_mem):
    n_tensor = lax.axis_size("tensor")
    n_rows = lax.axis_size("rows")
    chips = n_tensor // 2
    tensor_index = lax.axis_index("tensor").astype(jnp.int32)
    row_index = lax.axis_index("rows").astype(jnp.int32)
    chip, core = tensor_index // 2, tensor_index % 2
    rows_dev, width = tokens.shape
    features = norm_gain.shape[0]
    kv_heads = w_key.shape[1] // HD
    sharers = n_tensor // kv_heads

    def to_core(x):
        return lax.ppermute(x, "tensor", [(i, i ^ 1) for i in range(n_tensor)])

    def to_chip(x, ahead):
        pairs = [(i, (i + 2 * ahead) % n_tensor) for i in range(n_tensor)]
        return lax.ppermute(x, "tensor", pairs)

    def up(x):
        return lax.ppermute(x, "rows", [(i, (i + 1) % n_rows) for i in range(n_rows)])

    away = range(1, chips)

    half_rows = rows_dev // HALVES
    sizes = [half_rows] * HALVES
    *pieces, own_tokens, stat = prep(tokens, sizes)
    chip_stats = [to_chip(stat, ahead) for ahead in away]
    stats = [stat, to_core(stat)] + chip_stats + [to_core(s) for s in chip_stats]

    def gather(piece):
        arrived = [to_chip(piece, ahead) for ahead in away]
        return arrived + [to_core(a) for a in arrived]

    far_pieces = [gather(pieces[0])]
    core_tokens = to_core(tokens)
    near_order = jnp.stack([tensor_index, tensor_index ^ 1])
    far_order = [(tensor_index - 2 * ahead) % n_tensor for ahead in away]
    far_order += [((tensor_index ^ 1) - 2 * ahead) % n_tensor for ahead in away]
    far_order = jnp.stack(far_order)

    head_group = after(tensor_index // sharers, stat)
    memories = [lax.dynamic_slice_in_dim(res_mem[0], head_group * HD, HD, 2)]
    for _ in range(n_rows - 1):
        memories.append(up(memories[-1]))

    half_dim = HD // 2
    lane = jnp.arange(HD, dtype=jnp.int32)
    frequency = rope_base ** (-((lane % half_dim).astype(f32) / half_dim))
    positions = (row_index * rows_dev + jnp.arange(rows_dev, dtype=jnp.int32)).astype(f32)
    angles = positions[:, None] * frequency[None, :]
    cosine = jnp.cos(angles)
    sine = jnp.sin(angles) * jnp.where(lane < half_dim, -1.0, 1.0)[None, :]

    gain = norm_gain.astype(f32)[None]
    targets = jnp.arange(chips, dtype=jnp.int32) * 2
    heads = [(targets + core) // sharers, (targets + 1 - core) // sharers, tensor_index[None]]
    scalars = jnp.concatenate(heads).astype(jnp.int32)
    held = load([after(w_key, stat), w_value])
    own, send = kv_partial(scalars, stats, gain, own_tokens, *held, chips)
    arrived = after(to_core(after(send, memories[1])), *far_pieces[0][: chips - 1])
    pairs = []
    for ahead in away:
        target = (chip + ahead) % chips
        pair = lax.dynamic_index_in_dim(own, target, 0, False).astype(f32)
        pair = pair + lax.dynamic_index_in_dim(arrived, target, 0, False).astype(f32)
        pairs.append(pair.astype(bf16))
    others = [to_chip(pair, ahead) for pair, ahead in zip(pairs, away)]
    targets = []
    for ahead in away:
        far = ((chip + ahead) % chips) * 2
        targets += [far + 1 - core, far + core]
    far_targets = jnp.stack(targets)
    near_targets = jnp.stack([tensor_index ^ 1, tensor_index])
    total_rows = n_rows * rows_dev
    longest = total_rows // 2
    back = -(-(longest - 1) // rows_dev)

    padded = jnp.concatenate([jnp.full((back * rows_dev,), -1, jnp.int32), doc_ids])
    k_doc = lax.dynamic_slice_in_dim(padded, row_index * rows_dev, (back + 1) * rows_dev)[None]
    q_doc = jnp.broadcast_to(k_doc[0, back * rows_dev :, None], (rows_dev, HD))
    pick = jnp.concatenate([row_index[None], res_len, assign[:, 0]])
    far_order = jnp.concatenate([far_order, near_targets])
    small = (k_doc, q_doc, pick, near_order, far_order, cosine, sine)

    w_out_far = load_columns(after(far_targets, *pairs, *small), w_out, width, n_tensor - 2)
    kv = [kv_final(own, arrived, others, cosine, sine, after(chip, w_out_far, *memories[2:3]))]
    last_piece = after(pieces[-1], kv[0])
    last_arrived = [to_chip(last_piece, ahead) for ahead in away]
    near_order = after(near_order, kv[0])
    near = query_near(near_order, stats, gain, own_tokens, core_tokens, w_query)
    for at in range(back):
        kv.insert(0, up(after(kv[0], near) if at == 1 else kv[0]))

    cuts = [half_rows], [half_rows]
    weights, ready, attended, outs = [w_query], [near], [], []
    for half in range(HALVES):
        if half == 1:
            arrived = [after(a, attended[0]) for a in last_arrived]
            far_pieces.append(last_arrived + [to_core(a) for a in arrived])
        sources = [list(x) for x in zip(*(far_pieces[half : half + 1]))]
        order = after(far_order, *ready)
        query, w_held = query_far(
            half, order, stats, gain, near, sources, weights, width, cosine, sine
        )
        weights = [w_held, w_out]
        one = attend_half(half, pick, query, q_doc, k_doc, kv, memories)
        attended.append(one)
        one = after(one, *(last_arrived if half == 0 else ()))
        ready, sums, begin = [], [[] for _ in cuts[half]], 0
        others, spacer = [], []
        for ahead in away:
            block = 2 * (ahead - 1)
            sent = project([one], w_out_far, block, width, cuts[half])
            last = after(attended[-1], *sent)
            others.append([to_core(x) for x in sent])
        if half == HALVES - 1:
            terms = project(attended[:-1] + [last], w_held, 0, width, [half_rows] * HALVES)
            one = after(one, *terms)
            spacer = [to_core(after(stat, *outs[0], *terms))]
            terms = [to_core(x) for x in terms]
        for at, size in enumerate(cuts[half]):
            for ahead, other in zip(away, others):
                (pair,) = project(
                    [one], w_out_far, 2 * ahead - 1, width, [size], added=[other[at]], begin=begin,
                    spacer=spacer,
                )
                ready.append(pair)
                sums[at].append(to_chip(pair, ahead))
            begin += size
        outs += sums
    sizes = list(cuts[0]) + list(cuts[1])
    own_half = after(attended[-1], *ready)
    parts = list(project([attended[0], own_half], w_held, 1, width, sizes, f32, terms))
    for at, arrived in enumerate(outs):
        for piece in arrived:
            parts[at] = parts[at] + piece.astype(f32)
    return jnp.concatenate([part.astype(bf16) for part in parts], 0)


def solution(mesh):
    in_specs = (
        P(("groups", "rows"), "tensor"),
        P(),
        P(None, "tensor"),
        P("tensor", None),
        P("tensor", None),
        P("tensor", None),
        P("groups"),
        P("groups", None),
        P("groups"),
        P(("groups", "rows"), None, None, None),
    )
    out_specs = P(("groups", "rows"), "tensor")
    return jax.shard_map(
        on_device, mesh=mesh, in_specs=in_specs, out_specs=out_specs, check_vma=False
    )
```
